256 devices in a mesh: group: 32 (over x_lo, z, core), inner: 8 (over y, x_hi).
Axes of the slice: x: 4 (x_hi: 2, x_lo: 2; x = x_hi * 2 + x_lo), y: 4, z: 8, core: 2. Of those that a mesh axis runs over, the one named last changes fastest.
Arguments:
- image_emb: bfloat16 [32768, 576], P(('group', 'inner')), may hold values from -8 to 8
- text_feat: bfloat16 [32768, 576], P(('group', 'inner')), may hold values from -8 to 8
- text_head: bfloat16 [576, 576], replicated, may hold values from -1 to 2
- pair_ids: int32 [32768], replicated, may hold values from 0 to 229375, as said below
- logit_scale: float32 [1], replicated, may hold values from 10 to 20
- logit_bias: float32 [1], replicated, may hold values from -8 to -4
Outputs:
- row_loss: float32 [32768], P(('group', 'inner'))
- image_grad: float32 [32768, 576], P(('group', 'inner'))
- text_grad: float32 [32768, 576], P(('group', 'inner'))
- head_grad: float32 [576, 576], replicated
The draws below stay inside these ranges and needn't reach their ends.
Inputs may be any that keep to these rules, and one draw needn't show every extreme that they name: `pair_ids`: an image and a text match exactly where their ids are equal; every image matches its own text.
All inputs are finite; a program needn't handle non-finite values.
Results may differ from the reference program's by a relative error of at most 0.00115.
The reference program's roundings to bfloat16 on the way (of `img_unit`, `txt_unit`, `coefficient` and `proj_grad`) count: a program that leaves them out, or rounds other values in their place, can miss the bound.
Values may be sent and summed in bfloat16 or wider, within the bound.
A program may use at most 128 MiB of HBM per device.

```python
import math
import jax
import jax.numpy as jnp
from jax import lax

D = 576
PAIRS = 32768


def draw_pair_ids(key, part):
    key = jax.random.fold_in(key, 11)
    positions = jnp.arange(PAIRS, dtype=jnp.int32)
    region = 6 * positions // PAIRS
    run_length = region + 1
    offsets = jax.random.randint(jax.random.fold_in(key, 1), (6,), 0, 6)
    offset = offsets[region] % run_length
    grouped = region * PAIRS + (positions + offset) // run_length
    single = jax.random.randint(jax.random.fold_in(key, 2), (PAIRS,), 0, 4) == 0
    single = single | (positions == PAIRS - 1)
    return jnp.where(single, 6 * PAIRS + positions, grouped).astype(jnp.int32)


def shared_parts(key, part):
    labels = draw_pair_ids(key, part)
    table = jax.random.normal(jax.random.fold_in(key, 21), (7 * PAIRS, 16), jnp.float32)
    latent = jnp.tile(table[labels], (1, D // 16))
    column_gain = jnp.clip(jax.random.normal(jax.random.fold_in(key, 22), (D,), jnp.float32), -3.0, 3.0)
    return (latent, column_gain)


def draw_image_emb(key, part):
    latent, column_gain = shared_parts(key, part)
    key = jax.random.fold_in(key, 3)
    noise = jax.random.normal(key, (PAIRS, D), jnp.float32)
    values = latent * column_gain[None, :] + 0.8 * noise
    return jnp.clip(values, -8.0, 8.0).astype(jnp.bfloat16)


def draw_text_feat(key, part):
    latent, column_gain = shared_parts(key, part)
    key = jax.random.fold_in(key, 4)
    noise = jax.random.normal(key, (PAIRS, D), jnp.float32)
    values = latent * column_gain[None, :] + 0.8 * noise
    return jnp.clip(values, -8.0, 8.0).astype(jnp.bfloat16)


def draw_text_head(key, part):
    key = jax.random.fold_in(key, 31)
    spread = jax.random.normal(key, (D, D), jnp.float32)
    values = jnp.eye(D, dtype=jnp.float32) + 0.5 * spread / math_sqrt(D)
    return jnp.clip(values, -1.0, 2.0).astype(jnp.bfloat16)


def math_sqrt(count):
    return float(count) ** 0.5


def setup_inputs(seed: int = 0) -> dict:
    arg_keys = jax.random.split(jax.random.key(seed), 7)
    image_emb = draw_image_emb(jax.random.fold_in(arg_keys[6], 71), 0)
    text_feat = draw_text_feat(jax.random.fold_in(arg_keys[6], 71), 0)
    text_head = draw_text_head(jax.random.fold_in(arg_keys[6], 71), 0)
    pair_ids = draw_pair_ids(jax.random.fold_in(arg_keys[6], 71), 0)
    logit_scale = jnp.clip(jax.random.uniform(arg_keys[4], (1,), jnp.float32, 10.0, 20.0), 10.0, 20.0)
    logit_bias = jnp.clip(jax.random.uniform(arg_keys[5], (1,), jnp.float32, -8.0, -4.0), -8.0, -4.0)
    return dict(image_emb=image_emb, text_feat=text_feat, text_head=text_head, pair_ids=pair_ids, logit_scale=logit_scale, logit_bias=logit_bias)


head_weight_scale = 16.0

def normalize(values):
    values_f = values.astype(jnp.float32)
    inv_norm = lax.rsqrt(lax.optimization_barrier(jnp.sum(values_f * values_f, axis=1, keepdims=True)) + 1e-06)
    return (values_f * inv_norm, inv_norm)

def normalize_back(upstream, unit_vals, inv_norm):
    return inv_norm * (upstream - unit_vals * lax.optimization_barrier(jnp.sum(unit_vals * upstream, axis=1, keepdims=True)))

def reference(image_emb, text_feat, text_head, pair_ids, logit_scale, logit_bias):
    logit_mult = logit_scale[0]
    logit_shift = logit_bias[0]
    img_unit_f, img_inv = normalize(image_emb)
    img_unit = img_unit_f.astype(jnp.bfloat16)
    proj = jnp.dot(text_feat, text_head, preferred_element_type=jnp.float32)
    txt_unit_f, txt_inv = normalize(proj)
    txt_unit = txt_unit_f.astype(jnp.bfloat16)
    block_rows = math.gcd(PAIRS, 512)
    block_count = PAIRS // block_rows
    img_blocks = img_unit.reshape(block_count, block_rows, D)
    id_blocks = pair_ids.reshape(block_count, block_rows)

    def one_block(carry_grad, block_pair):
        img_block, block_ids = block_pair
        logits = logit_mult * lax.dot_general(txt_unit, img_block, (((1,), (1,)), ((), ())), preferred_element_type=jnp.float32) + logit_shift
        label_sign = jnp.where(pair_ids[:, None] == block_ids[None, :], 1.0, -1.0)
        margin = -label_sign * logits
        loss_cols = lax.optimization_barrier(jnp.sum(jax.nn.softplus(margin), axis=0)) / PAIRS
        coefficient = (-label_sign * jax.nn.sigmoid(margin)).astype(jnp.bfloat16)
        img_part = logit_mult * lax.dot_general(coefficient, txt_unit, (((0,), (0,)), ((), ())), preferred_element_type=jnp.float32)
        carry_grad = carry_grad + logit_mult * jnp.dot(coefficient, img_block, preferred_element_type=jnp.float32)
        return (carry_grad, (img_part, loss_cols))
    txt_unit_grad, (img_parts, loss_parts) = lax.scan(one_block, jnp.zeros((PAIRS, D), jnp.float32), (img_blocks, id_blocks))
    img_unit_grad = img_parts.reshape(PAIRS, D)
    row_loss = loss_parts.reshape(PAIRS)
    image_grad = normalize_back(img_unit_grad, img_unit_f, img_inv)
    proj_grad = normalize_back(txt_unit_grad, txt_unit_f, txt_inv).astype(jnp.bfloat16)
    text_grad = lax.dot_general(proj_grad, text_head, (((1,), (1,)), ((), ())), preferred_element_type=jnp.float32)
    head_grad = head_weight_scale * lax.dot_general(text_feat, proj_grad, (((0,), (0,)), ((), ())), preferred_element_type=jnp.float32)
    return (row_loss, image_grad, text_grad, head_grad)
```

```python
import functools
import jax
import jax.numpy as jnp
from jax import lax
from jax.experimental import pallas as pl
from jax.experimental.pallas import tpu as pltpu
from jax.sharding import PartitionSpec as P

HEAD_SCALE = 16.0
LOG2E = 1.4426950408889634
D = 576
B = 128
GR = D + 8
HT = 384
f32 = jnp.float32
bf16 = jnp.bfloat16


def dg(a, b, ca, cb):
    return lax.dot_general(a, b, (((ca,), (cb,)), ((), ())), preferred_element_type=f32)


def coords():
    g = lax.axis_index("group")
    i = lax.axis_index("inner")
    return lax.rem(i, 2) * 2 + g // 16, i // 2, lax.rem(g // 2, 8), lax.rem(g, 2)


def mesh_id(x, y, z, c):
    return (lax.rem(x, 2) * 8 + z) * 2 + c, y * 2 + x // 2


def peer(kp=0, kq=0, kz=0, kc=0):
    x, y, z, c = coords()
    dx = jnp.where(c == 0, kp, kq)
    dy = jnp.where(c == 0, kq, kp)
    return mesh_id(
        lax.rem(x + dx + 4, 4), lax.rem(y + dy + 4, 4), lax.rem(z + kz + 8, 8), lax.rem(c + kc, 2)
    )


def remote(src, dst, ss, rs, **k):
    return pltpu.make_async_remote_copy(
        src_ref=src, dst_ref=dst, send_sem=ss, recv_sem=rs,
        device_id=peer(**k), device_id_type=pl.DeviceIdType.MESH,
    )


def unit_rows(v):
    inv = lax.rsqrt(jnp.sum(v * v, axis=1, keepdims=True) + 1e-06)
    return v * inv, inv


def normalize_back(up, unit, inv):
    return inv * (up - unit * jnp.sum(unit * up, axis=1, keepdims=True))


def score(dots, match, s2, b2):
    z = dots * s2 + b2
    m = jnp.where(match, -z, z)
    u = jnp.exp2(m)
    w = 1.0 + u
    r = 1.0 / w
    sg = u * r
    loss = jnp.log(w) + (u - (w - 1.0)) * r
    return loss, jnp.where(match, -sg, sg).astype(bf16)


def kernel(scale_ref, bias_ref, emb, feat, head, ids,
           loss_out, img_out, txt_out, head_out,
           imgT, img, txtT, idi, lacc, gi, gt, imgu, txtu, invs,
           rcore, rright, rleft, r1, r2, hp, hcore, hP, hQ, hz, res,
           s_ag, r_ag, s_rs, r_rs, s_ar, r_ar):
    x, y, z, c = coords()
    pp = jnp.where(c == 0, x, y)
    qq = jnp.where(c == 0, y, x)
    bar = pltpu.get_barrier_semaphore()
    partners = ([dict(kp=k) for k in (1, 2, 3)] + [dict(kq=k) for k in (1, 2, 3)]
                + [dict(kz=k) for k in range(1, 8)] + [dict(kc=1)])
    for k in partners:
        pl.semaphore_signal(bar, inc=1, device_id=peer(**k), device_id_type=pl.DeviceIdType.MESH)

    u, inv = unit_rows(emb[...].astype(f32))
    imgu[...] = u
    invs[0] = inv * jnp.ones((1, B), f32)
    imgT[0] = u.T.astype(bf16)
    v, vinv = unit_rows(jnp.dot(feat[...], head[...], preferred_element_type=f32))
    txtu[...] = v
    invs[1] = vinv * jnp.ones((1, B), f32)
    txtT[0, 0] = v.T.astype(bf16)
    pl.semaphore_wait(bar, len(partners))

    n = [0]

    def ag(src, dst, **k):
        j = n[0]
        n[0] += 1
        return remote(src, dst, s_ag.at[j], r_ag.at[j], **k)

    started = []

    def go(cp):
        cp.start()
        started.append(cp)
        return cp

    p_in = {k: go(ag(imgT.at[0], imgT.at[k], kp=k)) for k in (1, 3, 2)}
    right = go(ag(txtT.at[0, 0], txtT.at[7, 0], kz=1))
    left = go(ag(txtT.at[0, 0], txtT.at[1, 0], kz=-1))
    sib = [go(ag(txtT.at[0, 0], txtT.at[0, 1], kc=1))]
    q_in = [go(ag(imgT.at[0], imgT.at[4 * k], kq=k)) for k in (1, 3, 2)]

    gi[...] = jnp.zeros_like(gi)
    lacc[...] = jnp.zeros_like(lacc)

    def p_forward(j):
        p_in[j].wait_recv()
        for k in (1, 3, 2):
            q_in.append(go(ag(imgT.at[j], imgT.at[4 * k + j], kq=k)))

    def z_forward(s):
        nonlocal right, left
        right.wait_recv()
        a = 7 - s
        if s < 3:
            nxt = go(ag(txtT.at[a, 0], txtT.at[a - 1, 0], kz=1))
        sib.append(go(ag(txtT.at[a, 0], txtT.at[a, 1], kc=1)))
        if s < 3:
            right = nxt
            left.wait_recv()
            b = 1 + s
            if s < 2:
                left = go(ag(txtT.at[b, 0], txtT.at[b + 1, 0], kz=-1))
            sib.append(go(ag(txtT.at[b, 0], txtT.at[b, 1], kc=1)))

    p_forward(1)
    p_forward(3)
    z_forward(0)
    p_forward(2)
    z_forward(1)
    z_forward(2)
    z_forward(3)
    for cp in q_in + sib:
        cp.wait_recv()

    def block_prep(b, _):
        kq = b // 4
        kp = lax.rem(b, 4)
        gg, ii = peer(kp=-kp, kq=-kq)
        row = ids[pl.ds(gg * 8 + ii, 1), :]
        idi[b] = jnp.broadcast_to(row, (B, B)).T
        img[pl.ds(pl.multiple_of(b * B, B), B), :] = imgT[b].astype(f32).T.astype(bf16)
        return 0

    lax.fori_loop(0, 16, block_prep, 0)

    s2 = scale_ref[0] * LOG2E
    b2 = bias_ref[0] * LOG2E
    CH = 512

    def text_ids(j, s):
        gg, ii = mesh_id(x, y, lax.rem(z + j, 8), lax.rem(c + s, 2))
        return ids[pl.ds(gg * 8 + ii, 1), :]

    def core_copy(j):
        return remote(gt.at[j, 1], rcore.at[j], s_rs.at[j], r_rs.at[j], kc=1)

    def right_copy(t):
        return remote(gt.at[4 - t, 0], rright.at[t], s_rs.at[8 + t], r_rs.at[8 + t], kz=1)

    def left_copy(t):
        return remote(gt.at[4 + t, 0], rleft.at[t], s_rs.at[12 + t], r_rs.at[12 + t], kz=-1)

    def hand_on(t):
        core_copy(4 + t).wait_recv()
        gt[4 + t, 0] += rcore[4 + t]
        core_copy(3 - t).wait_recv()
        gt[3 - t, 0] += rcore[3 - t]

        @pl.when(t == 0)
        def _():
            right_copy(0).start()

        @pl.when(t > 0)
        def _():
            @pl.when(t > 1)
            def _():
                left_copy(t - 1).wait_recv()
                gt[4 + t, 0] += rleft[t - 1]
            left_copy(t).start()
            right_copy(t - 1).wait_recv()
            gt[4 - t, 0] += rright[t - 1]
            right_copy(t).start()

    def tile(t, _):
        ja = 4 + t
        jb = 3 - t
        tT = jnp.concatenate([txtT[ja, 0], txtT[ja, 1], txtT[jb, 0], txtT[jb, 1]], axis=1)
        idt = jnp.concatenate([text_ids(ja, 0), text_ids(ja, 1), text_ids(jb, 0), text_ids(jb, 1)], axis=1)

        def dots_of(ch):
            return jnp.dot(img[pl.ds(ch * CH, CH), :], tT, preferred_element_type=f32)

        def coef_of(ch, dots):
            ii = jnp.concatenate([idi[4 * ch + k] for k in range(4)], axis=0)
            match = jnp.concatenate([ii] * 4, axis=1) == idt
            loss, co = score(dots, match, s2, b2)
            part = (loss[:, :B] + loss[:, B:2 * B]) + (loss[:, 2 * B:3 * B] + loss[:, 3 * B:])
            lacc[pl.ds(ch * CH, CH), :] += part
            return co

        def grads_of(ch, co, acc):
            iT = jnp.concatenate([imgT[4 * ch + k] for k in range(4)], axis=1)
            g = jnp.dot(iT, co, preferred_element_type=f32)
            h = dg(tT, co, 1, 1)
            for k in range(4):
                gi[4 * ch + k, 0:D, :] += h[:, k * B:(k + 1) * B]
            return g if acc is None else acc + g

        nch = 4
        d = {0: dots_of(0)}
        co = {}
        acc = None
        for ch in range(nch + 1):
            if ch + 1 < nch:
                d[ch + 1] = dots_of(ch + 1)
            if ch < nch:
                co[ch] = coef_of(ch, d.pop(ch))
            if ch >= 1:
                acc = grads_of(ch - 1, co.pop(ch - 1), acc)
        gt[ja, 0] = acc[:, :B]
        gt[ja, 1] = acc[:, B:2 * B]
        gt[jb, 0] = acc[:, 2 * B:3 * B]
        gt[jb, 1] = acc[:, 3 * B:]
        core_copy(ja).start()
        core_copy(jb).start()

        @pl.when(t > 0)
        def _():
            hand_on(t - 1)
        return 0

    lax.fori_loop(0, 4, tile, 0)

    def r1_copy(k, j):
        i = (k - 1) * 4 + j
        return remote(gi.at[4 * k + j], r1.at[i], s_rs.at[16 + i], r_rs.at[16 + i], kq=-k)

    def r2_copy(k):
        return remote(gi.at[k], r2.at[k - 1], s_rs.at[28 + k], r_rs.at[28 + k], kp=-k)

    def loss_row(b, _):
        gi[b, D:GR, :] = jnp.broadcast_to(
            jnp.sum(lacc[pl.ds(pl.multiple_of(b * B, B), B), :].T, axis=0, keepdims=True), (8, B))
        return 0

    lax.fori_loop(0, 16, loss_row, 0)
    for j in (2, 1, 3, 0):
        for k in (2, 1, 3):
            r1_copy(k, j).start()

    hand_on(3)
    left_copy(3).wait_recv()
    right_copy(3).wait_recv()
    tg = ((gt[0, 0] + rleft[3]) + rright[3]) * scale_ref[0]
    pg = normalize_back(tg.T, txtu[...], invs[1][:, :1]).astype(bf16)
    txt_out[...] = dg(pg, head[...], 1, 1)
    part = HEAD_SCALE * dg(feat[...], pg, 0, 0)
    part = jnp.concatenate([part, jnp.zeros((D, 64), f32)], axis=1)
    for k in range(5):
        hp[72 * k:72 * (k + 1)] = part[:, k * B:(k + 1) * B].reshape(72, 8, B)
    hp[360:HT] = jnp.zeros((HT - 360, 8, B), f32)

    def ar(j, src, dst, **k):
        return remote(src, dst, s_ar.at[j], r_ar.at[j], **k)

    h0 = ar(0, hp.at[pl.ds((1 - c) * 192, 192)], hcore, kc=1)
    h0.start()

    def r1_sum(j):
        for k in (1, 2, 3):
            r1_copy(k, j).wait_recv()
            gi[j] += r1[(k - 1) * 4 + j]

    h0.wait()
    hcore[...] += hp[pl.ds(c * 192, 192)]
    hp_copies = []
    for k in (1, 2, 3):
        cp = ar(k, hcore.at[pl.ds(lax.rem(pp + k, 4) * 48, 48)], hP.at[k - 1], kp=k)
        cp.start()
        hp_copies.append(cp)
    for j in (2, 1, 3):
        r1_sum(j)
        r2_copy(j).start()
    r1_sum(0)
    for cp in hp_copies:
        cp.wait()
    hcore[pl.ds(pp * 48, 48)] += (hP[0] + hP[1]) + hP[2]
    hq_copies = []
    for k in (1, 2, 3):
        cp = ar(3 + k, hcore.at[pl.ds(pp * 48 + lax.rem(qq + k, 4) * 12, 12)], hQ.at[k - 1], kq=k)
        cp.start()
        hq_copies.append(cp)
    for k in (1, 2, 3):
        r2_copy(k).wait_recv()
    ig = (gi[0] + r2[0]) + (r2[1] + r2[2])
    loss_out[...] = ig[D:D + 1, :] / (256 * B)
    img_out[...] = normalize_back((ig[0:D, :] * scale_ref[0]).T, imgu[...], invs[0][:, :1])
    for cp in hq_copies:
        cp.wait()
    hz[z] = hcore[pl.ds(pp * 48 + qq * 12, 12)] + ((hQ[0] + hQ[1]) + hQ[2])
    hz_copies = []
    for k in range(1, 8):
        cp = ar(6 + k, hz.at[z], hz.at[z], kz=k)
        cp.start()
        hz_copies.append(cp)
    for cp in hz_copies:
        cp.wait()
    tot = hz[0]
    for k in range(1, 8):
        tot = tot + hz[k]
    base = c * 192 + pp * 48
    res[pl.ds(base + qq * 12, 12)] = tot
    cps = []
    for k in (1, 2, 3):
        sl = pl.ds(base + qq * 12, 12)
        cp = ar(13 + k, res.at[sl], res.at[sl], kq=k)
        cp.start()
        cps.append(cp)
    for cp in cps:
        cp.wait()
    cps = []
    for k in (1, 2, 3):
        sl = pl.ds(base, 48)
        cp = ar(16 + k, res.at[sl], res.at[sl], kp=k)
        cp.start()
        cps.append(cp)
    for cp in cps:
        cp.wait()
    sl = pl.ds(c * 192, 192)
    cp = ar(20, res.at[sl], res.at[sl], kc=1)
    cp.start()
    cp.wait()
    for k in range(5):
        w = min(B, D - k * B)
        head_out[:, k * B:k * B + w] = res[72 * k:72 * (k + 1)].reshape(D, B)[:, :w]

    for cp in started:
        cp.wait_send()
    for j in range(8):
        core_copy(j).wait_send()
    for t in range(4):
        right_copy(t).wait_send()
        if t:
            left_copy(t).wait_send()
    for j in range(4):
        for k in (1, 2, 3):
            r1_copy(k, j).wait_send()
    for k in (1, 2, 3):
        r2_copy(k).wait_send()


def shards(image_emb, text_feat, text_head, pair_ids, logit_scale, logit_bias):
    vm = pl.BlockSpec(memory_space=pltpu.VMEM)
    sm = pl.BlockSpec(memory_space=pltpu.SMEM)
    V = pltpu.VMEM
    ids = pair_ids.reshape(256, B).astype(f32)
    loss, img_g, txt_g, head_g = pl.pallas_call(
        kernel,
        in_specs=[sm, sm, vm, vm, vm, vm],
        out_specs=[vm, vm, vm, vm],
        out_shape=[
            jax.ShapeDtypeStruct((1, B), f32),
            jax.ShapeDtypeStruct((B, D), f32),
            jax.ShapeDtypeStruct((B, D), f32),
            jax.ShapeDtypeStruct((D, D), f32),
        ],
        scratch_shapes=[
            V((16, D, B), bf16), V((16 * B, D), bf16), V((8, 2, D, B), bf16), V((16, B, B), f32),
            V((16 * B, B), f32), V((16, GR, B), f32), V((8, 2, D, B), f32),
            V((B, D), f32), V((B, D), f32), V((2, B, B), f32),
            V((8, D, B), f32), V((4, D, B), f32), V((4, D, B), f32),
            V((12, GR, B), f32), V((3, GR, B), f32),
            V((HT, 8, B), f32), V((HT // 2, 8, B), f32), V((3, 48, 8, B), f32), V((3, 12, 8, B), f32),
            V((8, 12, 8, B), f32), V((HT, 8, B), f32),
            pltpu.SemaphoreType.DMA((32,)), pltpu.SemaphoreType.DMA((32,)),
            pltpu.SemaphoreType.DMA((32,)), pltpu.SemaphoreType.DMA((32,)),
            pltpu.SemaphoreType.DMA((24,)), pltpu.SemaphoreType.DMA((24,)),
        ],
        compiler_params=pltpu.CompilerParams(
            collective_id=0, has_side_effects=True, vmem_limit_bytes=60 * 2**20),
        name="pair_loss",
    )(logit_scale, logit_bias, image_emb, text_feat, text_head, ids)
    return loss.reshape(B), img_g, txt_g, head_g


def solution(mesh):
    return jax.shard_map(
        shards,
        mesh=mesh,
        in_specs=(P(("group", "inner"), None), P(("group", "inner"), None), P(), P(), P(), P()),
        out_specs=(
            P(("group", "inner")),
            P(("group", "inner"), None),
            P(("group", "inner"), None),
            P(),
        ),
        check_vma=False,
    )
```

```python
import jax
import jax.numpy as jnp
from jax import lax
from jax.experimental import pallas as pl
from jax.experimental.pallas import tpu as pltpu
from jax.sharding import PartitionSpec as P

HEAD_SCALE = 16.0
LOG2E = 1.4426950408889634
D = 576
B = 128
PR = 384
QR = 96
XR = 16
f32 = jnp.float32
bf16 = jnp.bfloat16


def dg(a, b, ca, cb):
    return lax.dot_general(a, b, (((ca,), (cb,)), ((), ())), preferred_element_type=f32)


def coords():
    g = lax.axis_index("group")
    i = lax.axis_index("inner")
    return lax.rem(i, 2) * 2 + g // 16, i // 2, lax.rem(g // 2, 8), lax.rem(g, 2)


def mesh_id(x, y, z, c):
    return (lax.rem(x, 2) * 8 + z) * 2 + c, y * 2 + x // 2


def peer(kp=0, kq=0, kz=0, kc=0):
    x, y, z, c = coords()
    dx = jnp.where(c == 0, kp, kq)
    dy = jnp.where(c == 0, kq, kp)
    return mesh_id(
        lax.rem(x + dx + 4, 4), lax.rem(y + dy + 4, 4), lax.rem(z + kz + 8, 8), lax.rem(c + kc, 2)
    )


def remote(src, dst, ss, rs, **k):
    return pltpu.make_async_remote_copy(
        src_ref=src, dst_ref=dst, send_sem=ss, recv_sem=rs,
        device_id=peer(**k), device_id_type=pl.DeviceIdType.MESH,
    )


def score(dots, match, s2, b2):
    z = dots * s2 + b2
    m = jnp.where(match, -z, z)
    u = jnp.exp2(m)
    w = 1.0 + u
    r = 1.0 / w
    sg = u * r
    loss = jnp.log(w) + (u - (w - 1.0)) * r
    return loss, jnp.where(match, -sg, sg).astype(bf16)


def coded(v):
    top = jnp.maximum(jnp.max(jnp.abs(v), axis=0, keepdims=True), 1e-30)
    return jnp.round(v * (32766.0 / top)).astype(jnp.int32).astype(jnp.int16), top * (1.0 / 32766.0)


def decoded(q, scale):
    return q.astype(jnp.int32).astype(f32) * scale


def packed(v):
    top = jnp.maximum(jnp.max(jnp.abs(v), axis=0, keepdims=True), 1e-30)
    k = jnp.ceil(jnp.log2(top) + 0.001) - 15.0
    q = jnp.clip(jnp.round(v * jnp.exp2(-k)), -32767.0, 32767.0)
    q = jnp.concatenate([q, jnp.broadcast_to(k, (XR, B))], axis=0)
    return q.astype(jnp.int32).astype(jnp.int16)


def unpacked(q):
    n = q.shape[0] - XR
    f = q.astype(jnp.int32).astype(f32)
    return f[:n] * jnp.exp2(f[n:n + 1])


def kernel(scale_ref, bias_ref, embT, featT, head, ids,
           misc, res,
           imgT, img, txtT, idi, lacc, cbuf, gi, gt, imgu, txtu, invs, fsib, pgs,
           rcore, rright, rleft, q1, q1s, c1, c1s, q2, q2s, c2, c2s, hp, hPs, hP, hQs, hQ, hz,
           s_ag, r_ag, s_rs, r_rs, s_ar, r_ar):
    x, y, z, c = coords()
    pp = jnp.where(c == 0, x, y)
    qq = jnp.where(c == 0, y, x)
    bar = pltpu.get_barrier_semaphore()
    partners = ([dict(kp=k) for k in (1, 2, 3)] + [dict(kq=k) for k in (1, 2, 3)]
                + [dict(kz=k) for k in range(1, 8)] + [dict(kc=1)])
    for k in partners:
        pl.semaphore_signal(bar, inc=1, device_id=peer(**k), device_id_type=pl.DeviceIdType.MESH)

    e = embT[...].astype(f32)
    inv = lax.rsqrt(jnp.sum(e * e, axis=0, keepdims=True) + 1e-06)
    imgu[...] = e * inv
    invs[0:1, :] = inv
    imgT[0] = (e * inv).astype(bf16)
    projT = dg(featT[...], head[...], 0, 0).T
    vinv = lax.rsqrt(jnp.sum(projT * projT, axis=0, keepdims=True) + 1e-06)
    txtu[...] = projT * vinv
    invs[8:9, :] = vinv
    txtT[0, 0] = (projT * vinv).astype(bf16)
    pl.semaphore_wait(bar, len(partners))

    n = [0]
    started = []

    def go(src, dst, **k):
        j = n[0]
        n[0] += 1
        cp = remote(src, dst, s_ag.at[j], r_ag.at[j], **k)
        cp.start()
        started.append(cp)
        return cp

    H = D // 2
    half = [pl.ds(0, H), pl.ds(H, H)]
    quick = {}

    def slot(h, a, b):
        return 4 * b + a if h == 0 else 4 * a + b

    def first(h, k):
        return dict(kp=k) if h == 0 else dict(kq=k)

    def second(h, k):
        return dict(kq=k) if h == 0 else dict(kp=k)

    def hop(h, src, dst, axis, k):
        s = slot(h, *src)
        d = slot(h, *dst)
        quick[h, dst] = go(imgT.at[s, half[h]], imgT.at[d, half[h]], **axis(h, k))

    def spread(h, a):
        hop(h, (a, 0), (a, 1), second, 1)
        hop(h, (a, 0), (a, 3), second, -1)

    def arrived(h, a, b):
        quick.pop((h, (a, b))).wait_recv()

    for h in (0, 1):
        hop(h, (0, 0), (1, 0), first, 1)
        hop(h, (0, 0), (3, 0), first, -1)
    z_right = {}
    z_left = {}
    for h in (0, 1):
        z_right[0, h] = go(txtT.at[0, 0, half[h]], txtT.at[7, 0, half[h]], kz=1)
        z_left[0, h] = go(txtT.at[0, 0, half[h]], txtT.at[1, 0, half[h]], kz=-1)
    spread(0, 0)
    spread(1, 0)
    sib = [go(txtT.at[0, 0], txtT.at[0, 1], kc=1), go(featT, fsib, kc=1)]

    lacc[...] = jnp.zeros_like(lacc)

    def id_prep(b, _):
        gg, ii = peer(kp=-lax.rem(b, 4), kq=-(b // 4))
        row = ids[pl.ds(gg * 8 + ii, 1), :].astype(f32)
        idi[b] = jnp.broadcast_to(row, (B, B)).T
        return 0

    lax.fori_loop(0, 16, id_prep, 0)

    def img_prep(b):
        img[pl.ds(pl.multiple_of(b * B, B), B), :] = imgT[b].astype(f32).T.astype(bf16)

    def z_forward(s):
        a = 7 - s
        b = 1 + s
        for h in (0, 1):
            if (s, h) in z_right:
                z_right[s, h].wait_recv()
                if s < 2 or (s == 2 and h == 0):
                    z_right[s + 1, h] = go(txtT.at[a, 0, half[h]], txtT.at[a - 1, 0, half[h]], kz=1)
            if (s, h) in z_left:
                z_left[s, h].wait_recv()
                if s < 2 or (s == 2 and h == 1):
                    z_left[s + 1, h] = go(txtT.at[b, 0, half[h]], txtT.at[b + 1, 0, half[h]], kz=-1)
        sib.append(go(txtT.at[a, 0], txtT.at[a, 1], kc=1))
        if s < 3:
            sib.append(go(txtT.at[b, 0], txtT.at[b, 1], kc=1))

    def far(h, a):
        if h == 0:
            arrived(h, a, 1)
            hop(h, (a, 1), (a, 2), second, 1)
        else:
            arrived(h, a, 3)
            hop(h, (a, 3), (a, 2), second, -1)

    arrived(0, 1, 0)
    hop(0, (1, 0), (2, 0), first, 1)
    spread(0, 1)
    arrived(1, 3, 0)
    hop(1, (3, 0), (2, 0), first, -1)
    spread(1, 3)
    arrived(0, 3, 0)
    spread(0, 3)
    arrived(1, 1, 0)
    spread(1, 1)
    z_forward(0)
    far(0, 0)
    far(1, 0)
    for h in (0, 1):
        arrived(h, 2, 0)
        spread(h, 2)
    z_forward(1)
    far(0, 1)
    far(1, 3)
    far(0, 3)
    far(1, 1)
    z_forward(2)
    far(0, 2)
    far(1, 2)
    near = [(h, d) for (h, d) in quick if 2 not in d]
    for h, d in near:
        arrived(h, *d)

    def near_prep(r, _):
        kp = lax.rem(r, 3)
        kq = r // 3
        img_prep(4 * (kq + kq // 2) + kp + kp // 2)
        return 0

    lax.fori_loop(0, 9, near_prep, 0)
    z_forward(3)
    for h, d in list(quick):
        arrived(h, *d)

    def far_prep(r, _):
        img_prep(8 + r)
        return 0

    def far_prep2(r, _):
        img_prep(4 * (r + r // 2) + 2)
        return 0

    lax.fori_loop(0, 4, far_prep, 0)
    lax.fori_loop(0, 3, far_prep2, 0)
    for cp in sib:
        cp.wait_recv()

    s2 = scale_ref[0] * LOG2E
    b2 = bias_ref[0] * LOG2E
    CH = 512

    def text_ids(j, s):
        gg, ii = mesh_id(x, y, lax.rem(z + j, 8), lax.rem(c + s, 2))
        return ids[pl.ds(gg * 8 + ii, 1), :].astype(f32)

    def core_copy(j):
        return remote(gt.at[j, 1], rcore.at[j], s_rs.at[j], r_rs.at[j], kc=1)

    def hslice(h):
        return pl.ds(h * H, H)

    def right_copy(t, h):
        i = 8 + 2 * t + h
        return remote(gt.at[4 - t, 0, hslice(h)], rright.at[t, hslice(h)], s_rs.at[i], r_rs.at[i], kz=1)

    def left_copy(t, h):
        i = 16 + 2 * t + h
        return remote(gt.at[4 + t, 0, hslice(h)], rleft.at[t, hslice(h)], s_rs.at[i], r_rs.at[i], kz=-1)

    def take_right(t, h):
        right_copy(t - 1, h).wait_recv()
        gt[4 - t, 0, hslice(h)] += rright[t - 1, hslice(h)]

    def take_left(t, h):
        left_copy(t - 1, h).wait_recv()
        gt[4 + t, 0, hslice(h)] += rleft[t - 1, hslice(h)]

    def cores(t):
        core_copy(4 + t).wait_recv()
        gt[4 + t, 0] += rcore[4 + t]
        core_copy(3 - t).wait_recv()
        gt[3 - t, 0] += rcore[3 - t]

    def between(t):
        @pl.when(t == 1)
        def _():
            cores(0)
            right_copy(0, 0).start()
            left_copy(0, 1).start()

        @pl.when(t == 2)
        def _():
            cores(1)
            right_copy(1, 1).start()
            left_copy(1, 0).start()

        @pl.when(t == 3)
        def _():
            cores(2)
            take_right(1, 0)
            right_copy(1, 0).start()
            take_left(1, 1)
            left_copy(1, 1).start()

    def chain(t):
        for h in (0, 1):
            take_right(t, 1 - h)
            right_copy(t, 1 - h).start()
            take_left(t, h)
            left_copy(t, h).start()

    def tile(t, _):
        ja = 4 + t
        jb = 3 - t
        tT = jnp.concatenate([txtT[ja, 0], txtT[ja, 1], txtT[jb, 0], txtT[jb, 1]], axis=1)
        idt = jnp.concatenate([text_ids(ja, 0), text_ids(ja, 1), text_ids(jb, 0), text_ids(jb, 1)], axis=1)

        def dots_of(ch):
            return jnp.dot(img[pl.ds(ch * CH, CH), :], tT, preferred_element_type=f32)

        def coef_of(ch, dots):
            ii = jnp.concatenate([idi[4 * ch + k] for k in range(4)], axis=0)
            match = jnp.concatenate([ii] * 4, axis=1) == idt
            loss, co = score(dots, match, s2, b2)
            part = (loss[:, :B] + loss[:, B:2 * B]) + (loss[:, 2 * B:3 * B] + loss[:, 3 * B:])
            lacc[pl.ds(ch * CH, CH), :] += part
            return co

        def grads_of(ch, co, acc):
            iT = jnp.concatenate([imgT[4 * ch + k] for k in range(4)], axis=1)
            cbuf[t, ch] = co
            g = jnp.dot(iT, co, preferred_element_type=f32)
            return g if acc is None else acc + g

        nch = 4
        d = {0: dots_of(0)}
        co = {}
        acc = None
        for ch in range(nch + 1):
            if ch + 1 < nch:
                d[ch + 1] = dots_of(ch + 1)
            if ch < nch:
                co[ch] = coef_of(ch, d.pop(ch))
            if ch == 0:
                between(t)
            if ch >= 1:
                acc = grads_of(ch - 1, co.pop(ch - 1), acc)
        gt[ja, 0] = acc[:, :B]
        gt[ja, 1] = acc[:, B:2 * B]
        core_copy(ja).start()
        gt[jb, 0] = acc[:, 2 * B:3 * B]
        gt[jb, 1] = acc[:, 3 * B:]
        core_copy(jb).start()
        return 0

    lax.fori_loop(0, 4, tile, 0)

    def r1_copy(k, j):
        i = (k - 1) * 4 + j
        return remote(c1.at[i], q1.at[i], s_rs.at[24 + i], r_rs.at[24 + i], kq=-k)

    def r1s_copy(k):
        i = 36 + k
        return remote(c1s.at[k - 1], q1s.at[k - 1], s_rs.at[i], r_rs.at[i], kq=-k)

    def r2_copy(k):
        i = 40 + k
        return remote(c2.at[k - 1], q2.at[k - 1], s_rs.at[i], r_rs.at[i], kp=-k)

    def r2s_copy(k):
        i = 44 + k
        return remote(c2s.at[k - 1], q2s.at[k - 1], s_rs.at[i], r_rs.at[i], kp=-k)

    def loss_of(b):
        return jnp.sum(lacc[pl.ds(pl.multiple_of(b * B, B), B), :].T, axis=0, keepdims=True)

    def encode(k):
        def one(j, _):
            q, sc = coded(gi[4 * k + j])
            c1[(k - 1) * 4 + j] = q
            c1s[k - 1, j, 0:1, :] = sc
            c1s[k - 1, j, 1:2, :] = loss_of(4 * k + j)
            r1_copy(k, j).start()
            return 0
        lax.fori_loop(0, 4, one, 0)
        r1s_copy(k).start()

    def image_part(ch):
        at = [b for t in range(4) for b in ((4 + t, 0), (4 + t, 1), (3 - t, 0), (3 - t, 1))]
        tT = jnp.concatenate([txtT[j, s] for j, s in at], axis=1)
        co = jnp.concatenate([cbuf[t, ch] for t in range(4)], axis=1)
        h = dg(tT, co, 1, 1)
        for k in range(4):
            gi[4 * ch + k] = h[:, k * B:(k + 1) * B]

    image_part(2)
    cores(3)
    encode(2)
    chain(2)
    image_part(1)
    encode(1)
    image_part(3)
    encode(3)
    chain(3)
    image_part(0)

    for h in (0, 1):
        left_copy(3, h).wait_recv()
        right_copy(3, h).wait_recv()
    tg = ((gt[0, 0] + rleft[3]) + rright[3]) * scale_ref[0]
    tu = txtu[...]
    pgT = (invs[8:9, :] * (tg - tu * jnp.sum(tu * tg, axis=0, keepdims=True))).astype(bf16)
    pgs[0] = pgT

    def ar(j, src, dst, **k):
        return remote(src, dst, s_ar.at[j], r_ar.at[j], **k)

    cp = ar(0, pgs.at[0], pgs.at[1], kc=1)
    cp.start()
    misc[D:2 * D, :] = jnp.dot(head[...], pgT, preferred_element_type=f32)
    cp.wait()
    rows = pl.ds(pl.multiple_of(c * H, 32), H)
    f2 = jnp.concatenate([featT[rows, :], fsib[rows, :]], axis=1)
    p2 = jnp.concatenate([pgs[0], pgs[1]], axis=1)
    part = HEAD_SCALE * dg(f2, p2, 1, 1)
    for k in range(4):
        hp[H * k:H * (k + 1), :] = part[:, k * B:(k + 1) * B]
    hp[4 * H:5 * H, :] = jnp.concatenate([part[:, 4 * B:], jnp.zeros((H, 64), f32)], axis=1)
    hp[5 * H:4 * PR, :] = jnp.zeros((4 * PR - 5 * H, B), f32)

    def hp_rows(p, q, n):
        return pl.ds(pl.multiple_of(p * PR + q * QR, 32), n)

    cps = []
    for k in (2, 1, 3):
        hPs[k - 1] = packed(hp[hp_rows(lax.rem(pp + k, 4), 0, PR), :])
        cp = ar(k, hPs.at[k - 1], hP.at[k - 1], kp=k)
        cp.start()
        cps.append(cp)

    for k in (1, 3, 2):
        r1s_copy(k).wait_recv()

    def r1_sum(j):
        v = gi[j]
        ls = loss_of(j)
        for k in (1, 3, 2):
            r1_copy(k, j).wait_recv()
            v = v + decoded(q1[(k - 1) * 4 + j], q1s[k - 1, j, 0:1, :])
            ls = ls + q1s[k - 1, j, 1:2, :]
        return v, ls

    for j in (2, 1, 3):
        v, ls = r1_sum(j)
        q, sc = coded(v)
        c2[j - 1] = q
        c2s[j - 1, 0:1, :] = sc
        c2s[j - 1, 1:2, :] = ls
        r2_copy(j).start()
        r2s_copy(j).start()
    for cp in cps:
        cp.wait()
    hp[hp_rows(pp, 0, PR), :] += (unpacked(hP[0]) + unpacked(hP[1])) + unpacked(hP[2])
    cps = []
    for k in (2, 1, 3):
        hQs[k - 1] = packed(hp[hp_rows(pp, lax.rem(qq + k, 4), QR), :])
        cp = ar(3 + k, hQs.at[k - 1], hQ.at[k - 1], kq=k)
        cp.start()
        cps.append(cp)
    v0, ls0 = r1_sum(0)
    for cp in cps:
        cp.wait()
    tot = hp[hp_rows(pp, qq, QR), :] + ((unpacked(hQ[0]) + unpacked(hQ[1])) + unpacked(hQ[2]))
    hz[z] = packed(tot)
    cps = []
    for k in (4, 3, 5, 2, 6, 1, 7):
        cp = ar(6 + k, hz.at[z], hz.at[z], kz=k)
        cp.start()
        cps.append(cp)

    for k in (1, 3, 2):
        r2s_copy(k).wait_recv()
        r2_copy(k).wait_recv()
        v0 = v0 + decoded(q2[k - 1], q2s[k - 1, 0:1, :])
        ls0 = ls0 + q2s[k - 1, 1:2, :]
    ig = v0 * scale_ref[0]
    iu = imgu[...]
    misc[0:D, :] = invs[0:1, :] * (ig - iu * jnp.sum(iu * ig, axis=0, keepdims=True))
    misc[2 * D:2 * D + 8, :] = jnp.broadcast_to(ls0 / (256 * B), (8, B))

    for cp in cps:
        cp.wait()
    tot = unpacked(hz[0])
    for k in range(1, 8):
        tot = tot + unpacked(hz[k])
    base = c * 16 + pp * 4
    res[base + qq] = packed(tot)
    cps = []
    for k in (2, 1, 3):
        cp = ar(20 + k, res.at[base + qq], res.at[base + qq], kq=k)
        cp.start()
        cps.append(cp)
    for cp in cps:
        cp.wait()
    own = pl.ds(base, 4)
    pcs = {}
    for k in (2, 1, 3):
        pcs[k] = ar(23 + k, res.at[own], res.at[own], kp=k)
        pcs[k].start()
    ccs = [ar(27, res.at[own], res.at[own], kc=1)]
    ccs[0].start()
    for k in (1, 3, 2):
        pcs[k].wait()
        sl = pl.ds(c * 16 + lax.rem(pp + 4 - k, 4) * 4, 4)
        cp = ar(27 + k, res.at[sl], res.at[sl], kc=1)
        cp.start()
        ccs.append(cp)
    for cp in ccs:
        cp.wait()

    for cp in started:
        cp.wait_send()
    for j in range(8):
        core_copy(j).wait_send()
    for t in range(4):
        for h in (0, 1):
            if t or h == 0:
                right_copy(t, h).wait_send()
            if t or h == 1:
                left_copy(t, h).wait_send()
    for k in (1, 2, 3):
        for j in range(4):
            r1_copy(k, j).wait_send()
        r1s_copy(k).wait_send()
        r2_copy(k).wait_send()
        r2s_copy(k).wait_send()


def write_out(misc, res, loss, img, txt, head):
    loss[...] = misc[2 * D:2 * D + 1, :]
    img[...] = misc[0:D, :]
    txt[...] = misc[D:2 * D, :]
    H = D // 2
    for c in range(2):
        half = jnp.concatenate([unpacked(res[16 * c + n]) for n in range(16)], axis=0)
        for k in range(5):
            w = min(B, D - k * B)
            head[c * H:(c + 1) * H, k * B:k * B + w] = half[k * H:(k + 1) * H, :w]


def shards(image_emb, text_feat, text_head, pair_ids, logit_scale, logit_bias):
    vm = pl.BlockSpec(memory_space=pltpu.VMEM)
    sm = pl.BlockSpec(memory_space=pltpu.SMEM)
    V = pltpu.VMEM
    i16 = jnp.int16
    dma = pltpu.SemaphoreType.DMA
    misc, res = pl.pallas_call(
        kernel,
        in_specs=[sm, sm, vm, vm, vm, vm],
        out_specs=[vm, vm],
        out_shape=[
            jax.ShapeDtypeStruct((2 * D + 8, B), f32),
            jax.ShapeDtypeStruct((32, QR + XR, B), i16),
        ],
        scratch_shapes=[
            V((16, D, B), bf16), V((16 * B, D), bf16), V((8, 2, D, B), bf16), V((16, B, B), f32),
            V((16 * B, B), f32), V((4, 4, 512, 512), bf16), V((16, D, B), f32), V((8, 2, D, B), f32),
            V((D, B), f32), V((D, B), f32), V((16, B), f32), V((D, B), bf16), V((2, D, B), bf16),
            V((8, D, B), f32), V((4, D, B), f32), V((4, D, B), f32),
            V((12, D, B), i16), V((3, 4, 8, B), f32), V((12, D, B), i16), V((3, 4, 8, B), f32),
            V((3, D, B), i16), V((3, 8, B), f32), V((3, D, B), i16), V((3, 8, B), f32),
            V((4 * PR, B), f32), V((3, PR + XR, B), i16), V((3, PR + XR, B), i16),
            V((3, QR + XR, B), i16), V((3, QR + XR, B), i16), V((8, QR + XR, B), i16),
            dma((56,)), dma((56,)), dma((48,)), dma((48,)), dma((32,)), dma((32,)),
        ],
        compiler_params=pltpu.CompilerParams(
            collective_id=0, has_side_effects=True, vmem_limit_bytes=60 * 2**20),
        name="pair_loss",
    )(logit_scale, logit_bias, image_emb.T, text_feat.T, text_head, pair_ids.reshape(256, B))
    loss, img_g, txt_g, head_g = pl.pallas_call(
        write_out,
        in_specs=[vm, vm],
        out_specs=[vm, vm, vm, vm],
        out_shape=[
            jax.ShapeDtypeStruct((1, B), f32),
            jax.ShapeDtypeStruct((D, B), f32),
            jax.ShapeDtypeStruct((D, B), f32),
            jax.ShapeDtypeStruct((D, D), f32),
        ],
        name="write_out",
    )(misc, res)
    return loss.reshape(B), img_g.T, txt_g.T, head_g


def solution(mesh):
    return jax.shard_map(
        shards,
        mesh=mesh,
        in_specs=(P(("group", "inner"), None), P(("group", "inner"), None), P(), P(), P(), P()),
        out_specs=(
            P(("group", "inner")),
            P(("group", "inner"), None),
            P(("group", "inner"), None),
            P(),
        ),
        check_vma=False,
    )
```

```python
import jax
import jax.numpy as jnp
from jax import lax
from jax.experimental import pallas as pl
from jax.experimental.pallas import tpu as pltpu
from jax.sharding import PartitionSpec as P

HEAD_SCALE = 16.0
LOG2E = 1.4426950408889634
D = 576
B = 128
PR = 384
QR = 96
XR = 16
f32 = jnp.float32
bf16 = jnp.bfloat16


def dg(a, b, ca, cb):
    return lax.dot_general(a, b, (((ca,), (cb,)), ((), ())), preferred_element_type=f32)


def coords():
    g = lax.axis_index("group")
    i = lax.axis_index("inner")
    return lax.rem(i, 2) * 2 + g // 16, i // 2, lax.rem(g // 2, 8), lax.rem(g, 2)


def mesh_id(x, y, z, c):
    return (lax.rem(x, 2) * 8 + z) * 2 + c, y * 2 + x // 2


def peer(kp=0, kq=0, kz=0, kc=0):
    x, y, z, c = coords()
    dx = jnp.where(c == 0, kp, kq)
    dy = jnp.where(c == 0, kq, kp)
    return mesh_id(
        lax.rem(x + dx + 4, 4), lax.rem(y + dy + 4, 4), lax.rem(z + kz + 8, 8), lax.rem(c + kc, 2)
    )


def remote(src, dst, ss, rs, **k):
    return pltpu.make_async_remote_copy(
        src_ref=src, dst_ref=dst, send_sem=ss, recv_sem=rs,
        device_id=peer(**k), device_id_type=pl.DeviceIdType.MESH,
    )


def score(dots, match, s2, b2):
    z = dots * s2 + b2
    m = jnp.where(match, -z, z)
    u = jnp.exp2(m)
    w = 1.0 + u
    r = 1.0 / w
    sg = u * r
    loss = jnp.log(w) + (u - (w - 1.0)) * r
    return loss, jnp.where(match, -sg, sg).astype(bf16)


def power(top):
    return jnp.ceil(jnp.log2(jnp.maximum(top, 1e-30)) + 0.001) - 15.0


def packed(v, a=None):
    k = power(jnp.max(jnp.abs(v), axis=0, keepdims=True))
    q = jnp.clip(jnp.round(v * jnp.exp2(-k)), -32767.0, 32767.0)
    if a is None:
        rest = jnp.broadcast_to(k, (XR, B))
    else:
        ka = power(jnp.abs(a))
        hi = jnp.clip(jnp.round(a * jnp.exp2(-ka)), -32767.0, 32767.0)
        lo = jnp.clip(jnp.round((a * jnp.exp2(-ka) - hi) * 32768.0), -32767.0, 32767.0)
        i = lax.broadcasted_iota(jnp.int32, (XR, B), 0)
        rest = jnp.where(i == 0, k, jnp.where(i == 1, ka, jnp.where(i == 2, hi, lo)))
    return jnp.concatenate([q, rest], axis=0).astype(jnp.int32).astype(jnp.int16)


def unpacked(q):
    n = q.shape[0] - XR
    f = q.astype(jnp.int32).astype(f32)
    return f[:n] * jnp.exp2(f[n:n + 1])


def row_of(q):
    n = q.shape[0] - XR
    f = q[n:].astype(jnp.int32).astype(f32)
    return (f[2:3] + f[3:4] * (1.0 / 32768.0)) * jnp.exp2(f[1:2])


def kernel(scale_ref, bias_ref, embT, featT, head, ids,
           misc, res,
           imgT, img, txtT, idi, lacc, cbuf, gi, gt, imgu, txtu, invs, fsib, pgs,
           rcore, along, sright, sleft, rright, rleft, sa, ra, sb, rb, slo, rlo, sc, rc, sm, rm, hp, hPs, hP, hQs, hQ, hz,
           s_ag, r_ag, s_rs, r_rs, s_ar, r_ar):
    x, y, z, c = coords()
    pp = jnp.where(c == 0, x, y)
    qq = jnp.where(c == 0, y, x)
    bar = pltpu.get_barrier_semaphore()
    partners = ([dict(kp=k) for k in (1, 2, 3)] + [dict(kq=k) for k in (1, 2, 3)]
                + [dict(kz=k) for k in range(1, 8)] + [dict(kc=1)])
    for k in partners:
        pl.semaphore_signal(bar, inc=1, device_id=peer(**k), device_id_type=pl.DeviceIdType.MESH)

    e = embT[...].astype(f32)
    inv = lax.rsqrt(jnp.sum(e * e, axis=0, keepdims=True) + 1e-06)
    imgu[...] = e * inv
    invs[0:1, :] = inv
    imgT[0] = (e * inv).astype(bf16)
    projT = dg(featT[...], head[...], 0, 0).T
    vinv = lax.rsqrt(jnp.sum(projT * projT, axis=0, keepdims=True) + 1e-06)
    txtu[...] = projT * vinv
    invs[8:9, :] = vinv
    txtT[0, 0] = (projT * vinv).astype(bf16)
    pl.semaphore_wait(bar, len(partners))

    n = [0]
    started = []

    def go(src, dst, **k):
        j = n[0]
        n[0] += 1
        cp = remote(src, dst, s_ag.at[j], r_ag.at[j], **k)
        cp.start()
        started.append(cp)
        return cp

    H = D // 2
    half = [pl.ds(0, H), pl.ds(H, H)]
    quick = {}

    def slot(h, a, b):
        return 4 * b + a if h == 0 else 4 * a + b

    def first(h, k):
        return dict(kp=k) if h == 0 else dict(kq=k)

    def second(h, k):
        return dict(kq=k) if h == 0 else dict(kp=k)

    def hop(h, src, dst, axis, k):
        s = slot(h, *src)
        d = slot(h, *dst)
        quick[h, dst] = go(imgT.at[s, half[h]], imgT.at[d, half[h]], **axis(h, k))

    def spread(h, a):
        hop(h, (a, 0), (a, 1), second, 1)
        hop(h, (a, 0), (a, 3), second, -1)

    def arrived(h, a, b):
        quick.pop((h, (a, b))).wait_recv()

    for h in (0, 1):
        hop(h, (0, 0), (1, 0), first, 1)
        hop(h, (0, 0), (3, 0), first, -1)
    z_right = {}
    z_left = {}
    for h in (0, 1):
        z_right[0, h] = go(txtT.at[0, 0, half[h]], txtT.at[7, 0, half[h]], kz=1)
        z_left[0, h] = go(txtT.at[0, 0, half[h]], txtT.at[1, 0, half[h]], kz=-1)
    spread(0, 0)
    spread(1, 0)
    sib = [go(txtT.at[0, 0], txtT.at[0, 1], kc=1), go(featT, fsib, kc=1)]

    lacc[...] = jnp.zeros_like(lacc)

    def id_prep(b, _):
        gg, ii = peer(kp=-lax.rem(b, 4), kq=-(b // 4))
        row = ids[pl.ds(gg * 8 + ii, 1), :].astype(f32)
        idi[b] = jnp.broadcast_to(row, (B, B)).T
        return 0

    lax.fori_loop(0, 16, id_prep, 0)

    s2 = scale_ref[0] * LOG2E
    b2 = bias_ref[0] * LOG2E
    CH = 512

    def text_ids(j, s):
        gg, ii = mesh_id(x, y, lax.rem(z + j, 8), lax.rem(c + s, 2))
        return ids[pl.ds(gg * 8 + ii, 1), :].astype(f32)

    def text_tile(t):
        at = [(4 + t, 0), (4 + t, 1), (3 - t, 0), (3 - t, 1)]
        return (jnp.concatenate([txtT[j, s] for j, s in at], axis=1),
                jnp.concatenate([text_ids(j, s) for j, s in at], axis=1))

    def dots_of(ch, tT):
        return jnp.dot(img[pl.ds(ch * CH, CH), :], tT, preferred_element_type=f32)

    def coef_of(ch, dots, idt):
        ii = jnp.concatenate([idi[4 * ch + k] for k in range(4)], axis=0)
        match = jnp.concatenate([ii] * 4, axis=1) == idt
        loss, co = score(dots, match, s2, b2)
        part = (loss[:, :B] + loss[:, B:2 * B]) + (loss[:, 2 * B:3 * B] + loss[:, 3 * B:])
        lacc[pl.ds(ch * CH, CH), :] += part
        return co

    def score_early(t):
        tT, idt = text_tile(t)
        cbuf[t, 0] = coef_of(0, dots_of(0, tT), idt)

    def img_prep(b):
        img[pl.ds(pl.multiple_of(b * B, B), B), :] = imgT[b].astype(f32).T.astype(bf16)

    def z_forward(s):
        a = 7 - s
        b = 1 + s
        for h in (0, 1):
            if (s, h) in z_right:
                z_right[s, h].wait_recv()
                if s < 2 or (s == 2 and h == 0):
                    z_right[s + 1, h] = go(txtT.at[a, 0, half[h]], txtT.at[a - 1, 0, half[h]], kz=1)
            if (s, h) in z_left:
                z_left[s, h].wait_recv()
                if s < 2 or (s == 2 and h == 1):
                    z_left[s + 1, h] = go(txtT.at[b, 0, half[h]], txtT.at[b + 1, 0, half[h]], kz=-1)
        sib.append(go(txtT.at[a, 0], txtT.at[a, 1], kc=1))
        if s < 3:
            sib.append(go(txtT.at[b, 0], txtT.at[b, 1], kc=1))

    def far(h, a):
        if h == 0:
            arrived(h, a, 1)
            hop(h, (a, 1), (a, 2), second, 1)
        else:
            arrived(h, a, 3)
            hop(h, (a, 3), (a, 2), second, -1)

    arrived(0, 1, 0)
    hop(0, (1, 0), (2, 0), first, 1)
    spread(0, 1)
    arrived(1, 3, 0)
    hop(1, (3, 0), (2, 0), first, -1)
    spread(1, 3)
    arrived(0, 3, 0)
    spread(0, 3)
    arrived(1, 1, 0)
    spread(1, 1)
    z_forward(0)
    far(0, 0)
    far(1, 0)
    for h in (0, 1):
        arrived(h, 2, 0)
        spread(h, 2)
    z_forward(1)
    far(0, 1)
    far(1, 3)
    far(0, 3)
    far(1, 1)
    arrived(1, 0, 1)
    arrived(1, 0, 2)

    def own_prep(r, _):
        img_prep(r)
        return 0

    lax.fori_loop(0, 4, own_prep, 0)
    sib[0].wait_recv()
    sib[2].wait_recv()
    score_early(3)
    z_forward(2)
    far(0, 2)
    far(1, 2)
    sib[3].wait_recv()
    sib[4].wait_recv()
    score_early(2)
    near = [(h, d) for (h, d) in quick if 2 not in d]
    for h, d in near:
        arrived(h, *d)

    def near_prep(r, _):
        kp = lax.rem(r, 3)
        kq = r // 3
        img_prep(4 * (kq + kq // 2) + kp + kp // 2)
        return 0

    lax.fori_loop(3, 9, near_prep, 0)
    sib[5].wait_recv()
    sib[6].wait_recv()
    score_early(1)
    z_forward(3)
    for h, d in list(quick):
        arrived(h, *d)

    def far_prep(r, _):
        img_prep(8 + r)
        return 0

    def far_prep2(r, _):
        img_prep(4 * (r + r // 2) + 2)
        return 0

    lax.fori_loop(0, 4, far_prep, 0)
    lax.fori_loop(1, 3, far_prep2, 0)
    for n in (1, 7, 8):
        sib[n].wait_recv()
    score_early(0)

    def core_copy(j):
        return remote(gt.at[j, 1], rcore.at[j], s_rs.at[j], r_rs.at[j], kc=1)

    def hslice(h):
        return pl.ds(h * H, H)

    def right_copy(t, h):
        i = 8 + 2 * t + h
        return remote(sright.at[t, h], rright.at[t, h], s_rs.at[i], r_rs.at[i], kz=1)

    def left_copy(t, h):
        i = 16 + 2 * t + h
        return remote(sleft.at[t, h], rleft.at[t, h], s_rs.at[i], r_rs.at[i], kz=-1)

    def along_row(j):
        return along[pl.ds(j, 1), :]

    def send(buf, copy, t, j, h):
        buf[t, h] = packed(gt[j, 0, hslice(h)], along_row(j) if h == 0 else None)
        copy(t, h).start()

    def send_right(t, h):
        send(sright, right_copy, t, 4 - t, h)

    def send_left(t, h):
        send(sleft, left_copy, t, 4 + t, h)

    def take(buf, t, j, h):
        got = buf[t - 1, h]
        gt[j, 0, hslice(h)] += unpacked(got)
        if h == 0:
            along[pl.ds(j, 1), :] = along_row(j) + row_of(got)

    def take_right(t, h):
        right_copy(t - 1, h).wait_recv()
        take(rright, t, 4 - t, h)

    def take_left(t, h):
        left_copy(t - 1, h).wait_recv()
        take(rleft, t, 4 + t, h)

    def cores(t):
        for j in (4 + t, 3 - t):
            core_copy(j).wait_recv()
            g = gt[j, 0] + rcore[j]
            uj = txtT[j, 0].astype(f32)
            a = (jnp.sum(uj * g, axis=0, keepdims=True)
                 / jnp.maximum(jnp.sum(uj * uj, axis=0, keepdims=True), 1e-30))
            along[pl.ds(j, 1), :] = a
            gt[j, 0] = g - a * uj

    def chain(t):
        for h in (0, 1):
            take_right(t, 1 - h)
            send_right(t, 1 - h)
            take_left(t, h)
            send_left(t, h)

    def between(t, late):
        if not late:
            @pl.when(t == 1)
            def _():
                cores(0)
                send_right(0, 0)
                send_left(0, 1)

            @pl.when(t == 2)
            def _():
                cores(1)
                send_right(1, 1)
                send_left(1, 0)

            @pl.when(t == 3)
            def _():
                cores(2)
        else:
            @pl.when(t == 2)
            def _():
                take_right(1, 0)
                send_right(1, 0)
                take_left(1, 1)
                send_left(1, 1)

            @pl.when(t == 3)
            def _():
                chain(2)

    def tile(t, _):
        ja = 4 + t
        jb = 3 - t
        tT, idt = text_tile(t)

        def grads_of(ch, co, acc):
            iT = jnp.concatenate([imgT[4 * ch + k] for k in range(4)], axis=1)
            if ch:
                cbuf[t, ch] = co
            g = jnp.dot(iT, co, preferred_element_type=f32)
            return g if acc is None else acc + g

        nch = 4
        d = {1: dots_of(1, tT)}
        acc = grads_of(0, cbuf[t, 0], None)
        co = {}
        for ch in range(1, nch + 1):
            if ch + 1 < nch:
                d[ch + 1] = dots_of(ch + 1, tT)
            if ch < nch:
                co[ch] = coef_of(ch, d.pop(ch), idt)
            if ch == 1:
                between(t, False)
            if ch == 3:
                between(t, True)
            if ch >= 2:
                acc = grads_of(ch - 1, co.pop(ch - 1), acc)
        gt[ja, 0] = acc[:, :B]
        gt[ja, 1] = acc[:, B:2 * B]
        core_copy(ja).start()
        gt[jb, 0] = acc[:, 2 * B:3 * B]
        gt[jb, 1] = acc[:, 3 * B:]
        core_copy(jb).start()
        return 0

    lax.fori_loop(0, 4, tile, 0)

    def ra_copy(h, j):
        i = 24 + h * 4 + j
        return remote(sa.at[h, j], ra.at[h, j], s_rs.at[i], r_rs.at[i], kq=1 if h else -1)

    def rb_copy(h, j):
        i = 32 + h * 4 + j
        return remote(sb.at[h, j], rb.at[h, j], s_rs.at[i], r_rs.at[i], kq=1 if h else -1)

    def rl_copy(k):
        i = 39 + k
        return remote(slo.at[k - 1], rlo.at[k - 1], s_rs.at[i], r_rs.at[i], kq=-k)

    def rc_copy(k):
        i = 42 + k
        return remote(sc.at[k - 1], rc.at[k - 1], s_rs.at[i], r_rs.at[i], kp=-k)

    def rm_copy(k):
        i = 45 + k
        return remote(sm.at[k - 1], rm.at[k - 1], s_rs.at[i], r_rs.at[i], kp=-k)

    def loss_of(b):
        return jnp.sum(lacc[pl.ds(pl.multiple_of(b * B, B), B), :].T, axis=0, keepdims=True)

    def send_far():
        def one(j, _):
            for h in (0, 1):
                sa[h, j] = packed(gi[8 + j, hslice(h)])
                ra_copy(h, j).start()
            return 0
        lax.fori_loop(0, 4, one, 0)

    def send_near(h):
        def one(j, _):
            b = 12 + j if h else 4 + j
            ra_copy(h, j).wait_recv()
            gi[b, hslice(h)] += unpacked(ra[h, j])
            sb[h, j] = packed(gi[b])
            rb_copy(h, j).start()
            return 0
        lax.fori_loop(0, 4, one, 0)

    def send_losses():
        for k in (1, 2, 3):
            def one(j, _):
                slo[k - 1, pl.ds(j, 1), :] = loss_of(4 * k + j)
                return 0
            lax.fori_loop(0, 4, one, 0)
            rl_copy(k).start()

    def image_part(ch):
        at = [b for t in range(4) for b in ((4 + t, 0), (4 + t, 1), (3 - t, 0), (3 - t, 1))]
        tT = jnp.concatenate([txtT[j, s] for j, s in at], axis=1)
        co = jnp.concatenate([cbuf[t, ch] for t in range(4)], axis=1)
        h = dg(tT, co, 1, 1)
        for k in range(4):
            gi[4 * ch + k] = h[:, k * B:(k + 1) * B]

    image_part(2)
    send_far()
    image_part(1)
    image_part(3)
    cores(3)
    chain(3)
    send_near(0)
    send_near(1)

    for h in (0, 1):
        left_copy(3, h).wait_recv()
        right_copy(3, h).wait_recv()
    tg = jnp.concatenate([(gt[0, 0, hslice(h)] + unpacked(rleft[3, h])) + unpacked(rright[3, h]) for h in (0, 1)], axis=0)
    a = (along_row(0) + row_of(rleft[3, 0])) + row_of(rright[3, 0])
    tg = (tg + a * txtT[0, 0].astype(f32)) * scale_ref[0]
    tu = txtu[...]
    pgT = (invs[8:9, :] * (tg - tu * jnp.sum(tu * tg, axis=0, keepdims=True))).astype(bf16)
    pgs[0] = pgT

    def ar(j, src, dst, **k):
        return remote(src, dst, s_ar.at[j], r_ar.at[j], **k)

    cp = ar(0, pgs.at[0], pgs.at[1], kc=1)
    cp.start()
    misc[D:2 * D, :] = jnp.dot(head[...], pgT, preferred_element_type=f32)
    cp.wait()
    rows = pl.ds(pl.multiple_of(c * H, 32), H)
    f2 = jnp.concatenate([featT[rows, :], fsib[rows, :]], axis=1)
    p2 = jnp.concatenate([pgs[0], pgs[1]], axis=1)
    part = HEAD_SCALE * dg(f2, p2, 1, 1)
    for k in range(4):
        hp[H * k:H * (k + 1), :] = part[:, k * B:(k + 1) * B]
    hp[4 * H:5 * H, :] = jnp.concatenate([part[:, 4 * B:], jnp.zeros((H, 64), f32)], axis=1)
    hp[5 * H:4 * PR, :] = jnp.zeros((4 * PR - 5 * H, B), f32)

    def hp_rows(p, q, n):
        return pl.ds(pl.multiple_of(p * PR + q * QR, 32), n)

    cps = []
    for k in (2, 1, 3):
        hPs[k - 1] = packed(hp[hp_rows(lax.rem(pp + k, 4), 0, PR), :])
        cp = ar(k, hPs.at[k - 1], hP.at[k - 1], kp=k)
        cp.start()
        cps.append(cp)

    image_part(0)
    send_losses()
    for cp in cps:
        cp.wait()
    hp[hp_rows(pp, 0, PR), :] += (unpacked(hP[0]) + unpacked(hP[1])) + unpacked(hP[2])
    cps = []
    for k in (2, 1, 3):
        hQs[k - 1] = packed(hp[hp_rows(pp, lax.rem(qq + k, 4), QR), :])
        cp = ar(3 + k, hQs.at[k - 1], hQ.at[k - 1], kq=k)
        cp.start()
        cps.append(cp)

    for cp in cps:
        cp.wait()
    tot = hp[hp_rows(pp, qq, QR), :] + ((unpacked(hQ[0]) + unpacked(hQ[1])) + unpacked(hQ[2]))
    hz[z] = packed(tot)
    cps = []
    for k in (4, 3, 5, 2, 6, 1, 7):
        cp = ar(6 + k, hz.at[z], hz.at[z], kz=k)
        cp.start()
        cps.append(cp)

    for k in (1, 2, 3):
        rl_copy(k).wait_recv()

    def r1_sum(j):
        v = gi[j]
        for h in (0, 1):
            rb_copy(h, j).wait_recv()
            v = v + unpacked(rb[h, j])
        ls = (loss_of(j) + rlo[0, j:j + 1, :]) + (rlo[1, j:j + 1, :] + rlo[2, j:j + 1, :])
        return v, ls

    for j in (2, 1, 3):
        v, ls = r1_sum(j)
        sc[j - 1] = packed(v)
        rc_copy(j).start()
        sm[j - 1] = jnp.broadcast_to(ls, (8, B))
        rm_copy(j).start()
    v0, ls0 = r1_sum(0)
    for cp in cps:
        cp.wait()
    tot = unpacked(hz[0])
    for k in range(1, 8):
        tot = tot + unpacked(hz[k])
    base = c * 16 + pp * 4
    res[base + qq] = packed(tot)
    cps = []
    for k in (2, 1, 3):
        cp = ar(20 + k, res.at[base + qq], res.at[base + qq], kq=k)
        cp.start()
        cps.append(cp)
    for cp in cps:
        cp.wait()
    own = pl.ds(base, 4)
    pcs = {}
    for k in (2, 1, 3):
        pcs[k] = ar(23 + k, res.at[own], res.at[own], kp=k)
        pcs[k].start()
    ccs = [ar(27, res.at[own], res.at[own], kc=1)]
    ccs[0].start()
    for k in (1, 3, 2):
        rm_copy(k).wait_recv()
        rc_copy(k).wait_recv()
        v0 = v0 + unpacked(rc[k - 1])
        ls0 = ls0 + rm[k - 1, 0:1, :]
    ig = v0 * scale_ref[0]
    iu = imgu[...]
    misc[0:D, :] = invs[0:1, :] * (ig - iu * jnp.sum(iu * ig, axis=0, keepdims=True))
    misc[2 * D:2 * D + 8, :] = jnp.broadcast_to(ls0 / (256 * B), (8, B))
    for k in (1, 3, 2):
        pcs[k].wait()
        sl = pl.ds(c * 16 + lax.rem(pp + 4 - k, 4) * 4, 4)
        cp = ar(27 + k, res.at[sl], res.at[sl], kc=1)
        cp.start()
        ccs.append(cp)
    for cp in ccs:
        cp.wait()

    for cp in started:
        cp.wait_send()
    for j in range(8):
        core_copy(j).wait_send()
    for t in range(4):
        for h in (0, 1):
            if t or h == 0:
                right_copy(t, h).wait_send()
            if t or h == 1:
                left_copy(t, h).wait_send()
    for h in (0, 1):
        for j in range(4):
            ra_copy(h, j).wait_send()
            rb_copy(h, j).wait_send()
    for k in (1, 2, 3):
        rl_copy(k).wait_send()
        rc_copy(k).wait_send()
        rm_copy(k).wait_send()


def write_out(misc, res, loss, img, txt, head):
    loss[...] = misc[2 * D:2 * D + 1, :]
    img[...] = misc[0:D, :]
    txt[...] = misc[D:2 * D, :]
    H = D // 2
    for c in range(2):
        half = jnp.concatenate([unpacked(res[16 * c + n]) for n in range(16)], axis=0)
        for k in range(5):
            w = min(B, D - k * B)
            head[c * H:(c + 1) * H, k * B:k * B + w] = half[k * H:(k + 1) * H, :w]


def shards(image_emb, text_feat, text_head, pair_ids, logit_scale, logit_bias):
    vm = pl.BlockSpec(memory_space=pltpu.VMEM)
    sm = pl.BlockSpec(memory_space=pltpu.SMEM)
    V = pltpu.VMEM
    i16 = jnp.int16
    dma = pltpu.SemaphoreType.DMA
    misc, res = pl.pallas_call(
        kernel,
        in_specs=[sm, sm, vm, vm, vm, vm],
        out_specs=[vm, vm],
        out_shape=[
            jax.ShapeDtypeStruct((2 * D + 8, B), f32),
            jax.ShapeDtypeStruct((32, QR + XR, B), i16),
        ],
        scratch_shapes=[
            V((16, D, B), bf16), V((16 * B, D), bf16), V((8, 2, D, B), bf16), V((16, B, B), f32),
            V((16 * B, B), f32), V((4, 4, 512, 512), bf16), V((16, D, B), f32), V((8, 2, D, B), f32),
            V((D, B), f32), V((D, B), f32), V((16, B), f32), V((D, B), bf16), V((2, D, B), bf16),
            V((8, D, B), f32), V((8, B), f32),
            V((4, 2, D // 2 + XR, B), i16),
            V((4, 2, D // 2 + XR, B), i16),
            V((4, 2, D // 2 + XR, B), i16),
            V((4, 2, D // 2 + XR, B), i16),
            V((2, 4, D // 2 + XR, B), i16), V((2, 4, D // 2 + XR, B), i16),
            V((2, 4, D + XR, B), i16), V((2, 4, D + XR, B), i16),
            V((3, 8, B), f32), V((3, 8, B), f32),
            V((3, D + XR, B), i16), V((3, D + XR, B), i16), V((3, 8, B), f32), V((3, 8, B), f32),
            V((4 * PR, B), f32), V((3, PR + XR, B), i16), V((3, PR + XR, B), i16),
            V((3, QR + XR, B), i16), V((3, QR + XR, B), i16), V((8, QR + XR, B), i16),
            dma((56,)), dma((56,)), dma((52,)), dma((52,)), dma((32,)), dma((32,)),
        ],
        compiler_params=pltpu.CompilerParams(
            collective_id=0, has_side_effects=True, vmem_limit_bytes=60 * 2**20),
        name="pair_loss",
    )(logit_scale, logit_bias, image_emb.T, text_feat.T, text_head, pair_ids.reshape(256, B))
    loss, img_g, txt_g, head_g = pl.pallas_call(
        write_out,
        in_specs=[vm, vm],
        out_specs=[vm, vm, vm, vm],
        out_shape=[
            jax.ShapeDtypeStruct((1, B), f32),
            jax.ShapeDtypeStruct((D, B), f32),
            jax.ShapeDtypeStruct((D, B), f32),
            jax.ShapeDtypeStruct((D, D), f32),
        ],
        name="write_out",
    )(misc, res)
    return loss.reshape(B), img_g.T, txt_g.T, head_g


def solution(mesh):
    return jax.shard_map(
        shards,
        mesh=mesh,
        in_specs=(P(("group", "inner"), None), P(("group", "inner"), None), P(), P(), P(), P()),
        out_specs=(
            P(("group", "inner")),
            P(("group", "inner"), None),
            P(("group", "inner"), None),
            P(),
        ),
        check_vma=False,
    )
```

```python
import jax
import jax.numpy as jnp
from jax import lax
from jax.experimental import pallas as pl
from jax.experimental.pallas import tpu as pltpu
from jax.sharding import PartitionSpec as P

HEAD_SCALE = 16.0
LOG2E = 1.4426950408889634
D = 576
B = 128
PR = 384
QR = 96
XR = 16
f32 = jnp.float32
bf16 = jnp.bfloat16


def dg(a, b, ca, cb):
    return lax.dot_general(a, b, (((ca,), (cb,)), ((), ())), preferred_element_type=f32)


def coords():
    g = lax.axis_index("group")
    i = lax.axis_index("inner")
    return lax.rem(i, 2) * 2 + g // 16, i // 2, lax.rem(g // 2, 8), lax.rem(g, 2)


def mesh_id(x, y, z, c):
    return (lax.rem(x, 2) * 8 + z) * 2 + c, y * 2 + x // 2


def peer(kp=0, kq=0, kz=0, kc=0):
    x, y, z, c = coords()
    dx = jnp.where(c == 0, kp, kq)
    dy = jnp.where(c == 0, kq, kp)
    return mesh_id(
        lax.rem(x + dx + 4, 4), lax.rem(y + dy + 4, 4), lax.rem(z + kz + 8, 8), lax.rem(c + kc, 2)
    )


def remote(src, dst, ss, rs, **k):
    return pltpu.make_async_remote_copy(
        src_ref=src, dst_ref=dst, send_sem=ss, recv_sem=rs,
        device_id=peer(**k), device_id_type=pl.DeviceIdType.MESH,
    )


def score(dots, match, s2, b2):
    z = dots * s2 + b2
    m = jnp.where(match, -z, z)
    u = jnp.exp2(m)
    w = 1.0 + u
    r = 1.0 / w
    sg = u * r
    loss = jnp.log(w) + (u - (w - 1.0)) * r
    return loss, jnp.where(match, -sg, sg).astype(bf16)


def power(top):
    return jnp.ceil(jnp.log2(jnp.maximum(top, 1e-30)) + 0.001) - 15.0


def packed(v, a=None):
    k = power(jnp.max(jnp.abs(v), axis=0, keepdims=True))
    q = jnp.clip(jnp.round(v * jnp.exp2(-k)), -32767.0, 32767.0)
    if a is None:
        rest = jnp.broadcast_to(k, (XR, B))
    else:
        ka = power(jnp.abs(a))
        hi = jnp.clip(jnp.round(a * jnp.exp2(-ka)), -32767.0, 32767.0)
        lo = jnp.clip(jnp.round((a * jnp.exp2(-ka) - hi) * 32768.0), -32767.0, 32767.0)
        i = lax.broadcasted_iota(jnp.int32, (XR, B), 0)
        rest = jnp.where(i == 0, k, jnp.where(i == 1, ka, jnp.where(i == 2, hi, lo)))
    return jnp.concatenate([q, rest], axis=0).astype(jnp.int32).astype(jnp.int16)


def unpacked(q):
    n = q.shape[0] - XR
    f = q.astype(jnp.int32).astype(f32)
    return f[:n] * jnp.exp2(f[n:n + 1])


def row_of(q):
    n = q.shape[0] - XR
    f = q[n:].astype(jnp.int32).astype(f32)
    return (f[2:3] + f[3:4] * (1.0 / 32768.0)) * jnp.exp2(f[1:2])


def kernel(scale_ref, bias_ref, embT, featT, head, ids,
           misc, res,
           imgT, img, txtT, idi, lacc, cbuf, gi, gt, imgu, txtu, invs, fsib, pgs,
           rcore, along, sright, sleft, rright, rleft, sa, ra, sb, rb, slo, rlo, sc, rc, sm, rm, hp, hPs, hP, hQs, hQ, hz,
           s_ag, r_ag, s_rs, r_rs, s_ar, r_ar):
    x, y, z, c = coords()
    pp = jnp.where(c == 0, x, y)
    qq = jnp.where(c == 0, y, x)
    bar = pltpu.get_barrier_semaphore()
    partners = ([dict(kp=k) for k in (1, 2, 3)] + [dict(kq=k) for k in (1, 2, 3)]
                + [dict(kz=k) for k in range(1, 8)] + [dict(kc=1)])
    for k in partners:
        pl.semaphore_signal(bar, inc=1, device_id=peer(**k), device_id_type=pl.DeviceIdType.MESH)

    e = embT[...].astype(f32)
    inv = lax.rsqrt(jnp.sum(e * e, axis=0, keepdims=True) + 1e-06)
    imgu[...] = e * inv
    invs[0:1, :] = inv
    imgT[0] = (e * inv).astype(bf16)
    projT = dg(featT[...], head[...], 0, 0).T
    vinv = lax.rsqrt(jnp.sum(projT * projT, axis=0, keepdims=True) + 1e-06)
    txtu[...] = projT * vinv
    invs[8:9, :] = vinv
    txtT[0, 0] = (projT * vinv).astype(bf16)
    pl.semaphore_wait(bar, len(partners))

    n = [0]
    started = []

    def go(src, dst, **k):
        j = n[0]
        n[0] += 1
        cp = remote(src, dst, s_ag.at[j], r_ag.at[j], **k)
        cp.start()
        started.append(cp)
        return cp

    H = D // 2
    half = [pl.ds(0, H), pl.ds(H, H)]
    quick = {}

    def slot(h, a, b):
        return 4 * b + a if h == 0 else 4 * a + b

    def first(h, k):
        return dict(kp=k) if h == 0 else dict(kq=k)

    def second(h, k):
        return dict(kq=k) if h == 0 else dict(kp=k)

    def hop(h, src, dst, axis, k):
        s = slot(h, *src)
        d = slot(h, *dst)
        quick[h, dst] = go(imgT.at[s, half[h]], imgT.at[d, half[h]], **axis(h, k))

    def spread(h, a):
        hop(h, (a, 0), (a, 1), second, 1)
        hop(h, (a, 0), (a, 3), second, -1)

    def arrived(h, a, b):
        quick.pop((h, (a, b))).wait_recv()

    for h in (0, 1):
        hop(h, (0, 0), (1, 0), first, 1)
        hop(h, (0, 0), (3, 0), first, -1)
    z_right = {}
    z_left = {}
    for h in (0, 1):
        z_right[0, h] = go(txtT.at[0, 0, half[h]], txtT.at[7, 0, half[h]], kz=1)
        z_left[0, h] = go(txtT.at[0, 0, half[h]], txtT.at[1, 0, half[h]], kz=-1)
    spread(0, 0)
    spread(1, 0)
    sib = [go(txtT.at[0, 0], txtT.at[0, 1], kc=1), go(featT, fsib, kc=1)]

    lacc[...] = jnp.zeros_like(lacc)

    def id_prep(b, _):
        gg, ii = peer(kp=-lax.rem(b, 4), kq=-(b // 4))
        row = ids[pl.ds(gg * 8 + ii, 1), :].astype(f32)
        idi[b] = jnp.broadcast_to(row, (B, B)).T
        return 0

    lax.fori_loop(0, 16, id_prep, 0)

    s2 = scale_ref[0] * LOG2E
    b2 = bias_ref[0] * LOG2E
    CH = 512

    def text_ids(j, s):
        gg, ii = mesh_id(x, y, lax.rem(z + j, 8), lax.rem(c + s, 2))
        return ids[pl.ds(gg * 8 + ii, 1), :].astype(f32)

    def text_tile(t):
        at = [(4 + t, 0), (4 + t, 1), (3 - t, 0), (3 - t, 1)]
        return (jnp.concatenate([txtT[j, s] for j, s in at], axis=1),
                jnp.concatenate([text_ids(j, s) for j, s in at], axis=1))

    def dots_of(ch, tT):
        return jnp.dot(img[pl.ds(ch * CH, CH), :], tT, preferred_element_type=f32)

    def coef_of(ch, dots, idt):
        ii = jnp.concatenate([idi[4 * ch + k] for k in range(4)], axis=0)
        match = jnp.concatenate([ii] * 4, axis=1) == idt
        loss, co = score(dots, match, s2, b2)
        part = (loss[:, :B] + loss[:, B:2 * B]) + (loss[:, 2 * B:3 * B] + loss[:, 3 * B:])
        lacc[pl.ds(ch * CH, CH), :] += part
        return co

    def score_early(t):
        tT, idt = text_tile(t)
        cbuf[t, 0] = coef_of(0, dots_of(0, tT), idt)

    def img_prep(b):
        img[pl.ds(pl.multiple_of(b * B, B), B), :] = imgT[b].astype(f32).T.astype(bf16)

    def z_forward(s):
        a = 7 - s
        b = 1 + s
        for h in (0, 1):
            if (s, h) in z_right:
                z_right[s, h].wait_recv()
                if s < 2 or (s == 2 and h == 0):
                    z_right[s + 1, h] = go(txtT.at[a, 0, half[h]], txtT.at[a - 1, 0, half[h]], kz=1)
            if (s, h) in z_left:
                z_left[s, h].wait_recv()
                if s < 2 or (s == 2 and h == 1):
                    z_left[s + 1, h] = go(txtT.at[b, 0, half[h]], txtT.at[b + 1, 0, half[h]], kz=-1)
        sib.append(go(txtT.at[a, 0], txtT.at[a, 1], kc=1))
        if s < 3:
            sib.append(go(txtT.at[b, 0], txtT.at[b, 1], kc=1))

    def far(h, a):
        if h == 0:
            arrived(h, a, 1)
            hop(h, (a, 1), (a, 2), second, 1)
        else:
            arrived(h, a, 3)
            hop(h, (a, 3), (a, 2), second, -1)

    arrived(0, 1, 0)
    hop(0, (1, 0), (2, 0), first, 1)
    spread(0, 1)
    arrived(1, 3, 0)
    hop(1, (3, 0), (2, 0), first, -1)
    spread(1, 3)
    arrived(0, 3, 0)
    spread(0, 3)
    arrived(1, 1, 0)
    spread(1, 1)
    z_forward(0)
    far(0, 0)
    far(1, 0)
    for h in (0, 1):
        arrived(h, 2, 0)
        spread(h, 2)
    z_forward(1)
    far(0, 1)
    far(1, 3)
    far(0, 3)
    far(1, 1)
    arrived(1, 0, 1)
    arrived(1, 0, 2)

    def own_prep(r, _):
        img_prep(r)
        return 0

    lax.fori_loop(0, 4, own_prep, 0)
    sib[0].wait_recv()
    sib[2].wait_recv()
    score_early(3)
    z_forward(2)
    far(0, 2)
    far(1, 2)
    sib[3].wait_recv()
    sib[4].wait_recv()
    score_early(2)
    near = [(h, d) for (h, d) in quick if 2 not in d]
    for h, d in near:
        arrived(h, *d)

    def near_prep(r, _):
        kp = lax.rem(r, 3)
        kq = r // 3
        img_prep(4 * (kq + kq // 2) + kp + kp // 2)
        return 0

    lax.fori_loop(3, 9, near_prep, 0)
    sib[5].wait_recv()
    sib[6].wait_recv()
    score_early(1)
    z_forward(3)
    for h, d in list(quick):
        arrived(h, *d)

    def far_prep(r, _):
        img_prep(8 + r)
        return 0

    def far_prep2(r, _):
        img_prep(4 * (r + r // 2) + 2)
        return 0

    lax.fori_loop(0, 4, far_prep, 0)
    lax.fori_loop(1, 3, far_prep2, 0)
    for n in (1, 7, 8):
        sib[n].wait_recv()
    score_early(0)

    def core_copy(j):
        return remote(gt.at[j, 1], rcore.at[j], s_rs.at[j], r_rs.at[j], kc=1)

    def hslice(h):
        return pl.ds(h * H, H)

    def right_copy(t, h):
        i = 8 + 2 * t + h
        return remote(sright.at[t, h], rright.at[t, h], s_rs.at[i], r_rs.at[i], kz=1)

    def left_copy(t, h):
        i = 16 + 2 * t + h
        return remote(sleft.at[t, h], rleft.at[t, h], s_rs.at[i], r_rs.at[i], kz=-1)

    def along_row(j):
        return along[pl.ds(j, 1), :]

    def send(buf, copy, t, j, h):
        buf[t, h] = packed(gt[j, 0, hslice(h)], along_row(j) if h == 0 else None)
        copy(t, h).start()

    def send_right(t, h):
        send(sright, right_copy, t, 4 - t, h)

    def send_left(t, h):
        send(sleft, left_copy, t, 4 + t, h)

    def take(buf, t, j, h):
        got = buf[t - 1, h]
        gt[j, 0, hslice(h)] += unpacked(got)
        if h == 0:
            along[pl.ds(j, 1), :] = along_row(j) + row_of(got)

    def take_right(t, h):
        right_copy(t - 1, h).wait_recv()
        take(rright, t, 4 - t, h)

    def take_left(t, h):
        left_copy(t - 1, h).wait_recv()
        take(rleft, t, 4 + t, h)

    def cores(t):
        for j in (4 + t, 3 - t):
            core_copy(j).wait_recv()
            g = gt[j, 0] + rcore[j]
            uj = txtT[j, 0].astype(f32)
            a = (jnp.sum(uj * g, axis=0, keepdims=True)
                 / jnp.maximum(jnp.sum(uj * uj, axis=0, keepdims=True), 1e-30))
            along[pl.ds(j, 1), :] = a
            gt[j, 0] = g - a * uj

    def chain(t):
        for h in (0, 1):
            take_right(t, 1 - h)
            send_right(t, 1 - h)
            take_left(t, h)
            send_left(t, h)

    def between(t, late):
        if not late:
            @pl.when(t == 1)
            def _():
                cores(0)
                send_right(0, 0)
                send_left(0, 1)

            @pl.when(t == 2)
            def _():
                cores(1)
                send_right(1, 1)
                send_left(1, 0)

            @pl.when(t == 3)
            def _():
                cores(2)
        else:
            @pl.when(t == 2)
            def _():
                take_right(1, 0)
                send_right(1, 0)
                take_left(1, 1)
                send_left(1, 1)

            @pl.when(t == 3)
            def _():
                chain(2)

    def tile(t, _):
        ja = 4 + t
        jb = 3 - t
        tT, idt = text_tile(t)

        def grads_of(ch, co, acc):
            iT = jnp.concatenate([imgT[4 * ch + k] for k in range(4)], axis=1)
            if ch:
                cbuf[t, ch] = co
            g = jnp.dot(iT, co, preferred_element_type=f32)
            return g if acc is None else acc + g

        nch = 4
        d = {1: dots_of(1, tT)}
        acc = grads_of(0, cbuf[t, 0], None)
        co = {}
        for ch in range(1, nch + 1):
            if ch + 1 < nch:
                d[ch + 1] = dots_of(ch + 1, tT)
            if ch < nch:
                co[ch] = coef_of(ch, d.pop(ch), idt)
            if ch == 1:
                between(t, False)
            if ch == 3:
                between(t, True)
            if ch >= 2:
                acc = grads_of(ch - 1, co.pop(ch - 1), acc)
        gt[ja, 0] = acc[:, :B]
        gt[ja, 1] = acc[:, B:2 * B]
        core_copy(ja).start()
        gt[jb, 0] = acc[:, 2 * B:3 * B]
        gt[jb, 1] = acc[:, 3 * B:]
        core_copy(jb).start()
        return 0

    lax.fori_loop(0, 4, tile, 0)

    def ra_copy(h, j):
        i = 24 + h * 4 + j
        return remote(sa.at[h, j], ra.at[h, j], s_rs.at[i], r_rs.at[i], kq=1 if h else -1)

    def rb_copy(h, j):
        i = 32 + h * 4 + j
        return remote(sb.at[h, j], rb.at[h, j], s_rs.at[i], r_rs.at[i], kq=1 if h else -1)

    def rl_copy(k):
        i = 39 + k
        return remote(slo.at[k - 1], rlo.at[k - 1], s_rs.at[i], r_rs.at[i], kq=-k)

    def rc_copy(k):
        i = 42 + k
        return remote(sc.at[k - 1], rc.at[k - 1], s_rs.at[i], r_rs.at[i], kp=-k)

    def rm_copy(k):
        i = 45 + k
        return remote(sm.at[k - 1], rm.at[k - 1], s_rs.at[i], r_rs.at[i], kp=-k)

    def loss_of(b):
        return jnp.sum(lacc[pl.ds(pl.multiple_of(b * B, B), B), :].T, axis=0, keepdims=True)

    def send_far():
        def one(j, _):
            for h in (0, 1):
                sa[h, j] = packed(gi[8 + j, hslice(h)])
                ra_copy(h, j).start()
            return 0
        lax.fori_loop(0, 4, one, 0)

    def send_near(h):
        def one(j, _):
            b = 12 + j if h else 4 + j
            ra_copy(h, j).wait_recv()
            gi[b, hslice(h)] += unpacked(ra[h, j])
            sb[h, j] = packed(gi[b])
            rb_copy(h, j).start()
            return 0
        lax.fori_loop(0, 4, one, 0)

    def send_losses():
        for k in (1, 2, 3):
            def one(j, _):
                slo[k - 1, pl.ds(j, 1), :] = loss_of(4 * k + j)
                return 0
            lax.fori_loop(0, 4, one, 0)
            rl_copy(k).start()

    def image_part(ch):
        at = [b for t in range(4) for b in ((4 + t, 0), (4 + t, 1), (3 - t, 0), (3 - t, 1))]
        tT = jnp.concatenate([txtT[j, s] for j, s in at], axis=1)
        co = jnp.concatenate([cbuf[t, ch] for t in range(4)], axis=1)
        h = dg(tT, co, 1, 1)
        for k in range(4):
            gi[4 * ch + k] = h[:, k * B:(k + 1) * B]

    image_part(2)
    send_far()
    image_part(1)
    image_part(3)
    cores(3)
    chain(3)
    send_near(0)
    send_near(1)

    for h in (0, 1):
        left_copy(3, h).wait_recv()
        right_copy(3, h).wait_recv()
    tg = jnp.concatenate([(gt[0, 0, hslice(h)] + unpacked(rleft[3, h])) + unpacked(rright[3, h]) for h in (0, 1)], axis=0)
    a = (along_row(0) + row_of(rleft[3, 0])) + row_of(rright[3, 0])
    tg = (tg + a * txtT[0, 0].astype(f32)) * scale_ref[0]
    tu = txtu[...]
    pgT = (invs[8:9, :] * (tg - tu * jnp.sum(tu * tg, axis=0, keepdims=True))).astype(bf16)
    pgs[0] = pgT

    def ar(j, src, dst, **k):
        return remote(src, dst, s_ar.at[j], r_ar.at[j], **k)

    cp = ar(0, pgs.at[0], pgs.at[1], kc=1)
    cp.start()
    misc[D:2 * D, :] = jnp.dot(head[...], pgT, preferred_element_type=f32)
    cp.wait()
    rows = pl.ds(pl.multiple_of(c * H, 32), H)
    f2 = jnp.concatenate([featT[rows, :], fsib[rows, :]], axis=1)
    p2 = jnp.concatenate([pgs[0], pgs[1]], axis=1)
    part = HEAD_SCALE * dg(f2, p2, 1, 1)
    for k in range(4):
        hp[H * k:H * (k + 1), :] = part[:, k * B:(k + 1) * B]
    hp[4 * H:5 * H, :] = jnp.concatenate([part[:, 4 * B:], jnp.zeros((H, 64), f32)], axis=1)
    hp[5 * H:4 * PR, :] = jnp.zeros((4 * PR - 5 * H, B), f32)

    def hp_rows(p, q, n):
        return pl.ds(pl.multiple_of(p * PR + q * QR, 32), n)

    cps = []
    for k in (2, 1, 3):
        hPs[k - 1] = packed(hp[hp_rows(lax.rem(pp + k, 4), 0, PR), :])
        cp = ar(k, hPs.at[k - 1], hP.at[k - 1], kp=k)
        cp.start()
        cps.append(cp)

    image_part(0)
    send_losses()
    for cp in cps:
        cp.wait()
    hp[hp_rows(pp, 0, PR), :] += (unpacked(hP[0]) + unpacked(hP[1])) + unpacked(hP[2])
    cps = []
    for k in (2, 1, 3):
        hQs[k - 1] = packed(hp[hp_rows(pp, lax.rem(qq + k, 4), QR), :])
        cp = ar(3 + k, hQs.at[k - 1], hQ.at[k - 1], kq=k)
        cp.start()
        cps.append(cp)

    for cp in cps:
        cp.wait()
    tot = hp[hp_rows(pp, qq, QR), :] + ((unpacked(hQ[0]) + unpacked(hQ[1])) + unpacked(hQ[2]))
    hz[z] = packed(tot)
    cps = []
    for k in (4, 3, 5, 2, 6, 1, 7):
        cp = ar(6 + k, hz.at[z], hz.at[z], kz=k)
        cp.start()
        cps.append(cp)

    for k in (1, 2, 3):
        rl_copy(k).wait_recv()

    def r1_sum(j):
        v = gi[j]
        for h in (0, 1):
            rb_copy(h, j).wait_recv()
            v = v + unpacked(rb[h, j])
        ls = (loss_of(j) + rlo[0, j:j + 1, :]) + (rlo[1, j:j + 1, :] + rlo[2, j:j + 1, :])
        return v, ls

    for j in (2, 1, 3):
        v, ls = r1_sum(j)
        sc[j - 1] = packed(v)
        rc_copy(j).start()
        sm[j - 1] = jnp.broadcast_to(ls, (8, B))
        rm_copy(j).start()
    v0, ls0 = r1_sum(0)
    for cp in cps:
        cp.wait()
    tot = unpacked(hz[0])
    for k in range(1, 8):
        tot = tot + unpacked(hz[k])
    base = c * 16 + pp * 4
    res[base + qq] = packed(tot)
    q_back = {}
    for k in (2, 1, 3):
        q_back[k] = ar(20 + k, res.at[base + qq], res.at[base + qq], kq=k)
        q_back[k].start()
    pcs = {1: [], 2: [], 3: []}

    def p_back(n):
        at = base + lax.rem(qq + 4 - n, 4)
        for k in (2, 1, 3):
            cp = ar(28 + 4 * k + n, res.at[at], res.at[at], kp=k)
            cp.start()
            pcs[k].append(cp)

    p_back(0)
    for n in (1, 3, 2):
        q_back[n].wait()
        p_back(n)
    own = pl.ds(base, 4)
    ccs = [ar(27, res.at[own], res.at[own], kc=1)]
    ccs[0].start()
    for k in (1, 3, 2):
        rm_copy(k).wait_recv()
        rc_copy(k).wait_recv()
        v0 = v0 + unpacked(rc[k - 1])
        ls0 = ls0 + rm[k - 1, 0:1, :]
    ig = v0 * scale_ref[0]
    iu = imgu[...]
    misc[0:D, :] = invs[0:1, :] * (ig - iu * jnp.sum(iu * ig, axis=0, keepdims=True))
    misc[2 * D:2 * D + 8, :] = jnp.broadcast_to(ls0 / (256 * B), (8, B))
    for k in (1, 3, 2):
        for cp in pcs[k]:
            cp.wait()
        sl = pl.ds(c * 16 + lax.rem(pp + 4 - k, 4) * 4, 4)
        cp = ar(27 + k, res.at[sl], res.at[sl], kc=1)
        cp.start()
        ccs.append(cp)
    for cp in ccs:
        cp.wait()

    for cp in started:
        cp.wait_send()
    for j in range(8):
        core_copy(j).wait_send()
    for t in range(4):
        for h in (0, 1):
            if t or h == 0:
                right_copy(t, h).wait_send()
            if t or h == 1:
                left_copy(t, h).wait_send()
    for h in (0, 1):
        for j in range(4):
            ra_copy(h, j).wait_send()
            rb_copy(h, j).wait_send()
    for k in (1, 2, 3):
        rl_copy(k).wait_send()
        rc_copy(k).wait_send()
        rm_copy(k).wait_send()


def write_out(misc, res, loss, img, txt, head):
    loss[...] = misc[2 * D:2 * D + 1, :]
    img[...] = misc[0:D, :]
    txt[...] = misc[D:2 * D, :]
    H = D // 2
    for c in range(2):
        half = jnp.concatenate([unpacked(res[16 * c + n]) for n in range(16)], axis=0)
        for k in range(5):
            w = min(B, D - k * B)
            head[c * H:(c + 1) * H, k * B:k * B + w] = half[k * H:(k + 1) * H, :w]


def shards(image_emb, text_feat, text_head, pair_ids, logit_scale, logit_bias):
    vm = pl.BlockSpec(memory_space=pltpu.VMEM)
    sm = pl.BlockSpec(memory_space=pltpu.SMEM)
    V = pltpu.VMEM
    i16 = jnp.int16
    dma = pltpu.SemaphoreType.DMA
    misc, res = pl.pallas_call(
        kernel,
        in_specs=[sm, sm, vm, vm, vm, vm],
        out_specs=[vm, vm],
        out_shape=[
            jax.ShapeDtypeStruct((2 * D + 8, B), f32),
            jax.ShapeDtypeStruct((32, QR + XR, B), i16),
        ],
        scratch_shapes=[
            V((16, D, B), bf16), V((16 * B, D), bf16), V((8, 2, D, B), bf16), V((16, B, B), f32),
            V((16 * B, B), f32), V((4, 4, 512, 512), bf16), V((16, D, B), f32), V((8, 2, D, B), f32),
            V((D, B), f32), V((D, B), f32), V((16, B), f32), V((D, B), bf16), V((2, D, B), bf16),
            V((8, D, B), f32), V((8, B), f32),
            V((4, 2, D // 2 + XR, B), i16),
            V((4, 2, D // 2 + XR, B), i16),
            V((4, 2, D // 2 + XR, B), i16),
            V((4, 2, D // 2 + XR, B), i16),
            V((2, 4, D // 2 + XR, B), i16), V((2, 4, D // 2 + XR, B), i16),
            V((2, 4, D + XR, B), i16), V((2, 4, D + XR, B), i16),
            V((3, 8, B), f32), V((3, 8, B), f32),
            V((3, D + XR, B), i16), V((3, D + XR, B), i16), V((3, 8, B), f32), V((3, 8, B), f32),
            V((4 * PR, B), f32), V((3, PR + XR, B), i16), V((3, PR + XR, B), i16),
            V((3, QR + XR, B), i16), V((3, QR + XR, B), i16), V((8, QR + XR, B), i16),
            dma((56,)), dma((56,)), dma((52,)), dma((52,)), dma((48,)), dma((48,)),
        ],
        compiler_params=pltpu.CompilerParams(
            collective_id=0, has_side_effects=True, vmem_limit_bytes=60 * 2**20),
        name="pair_loss",
    )(logit_scale, logit_bias, image_emb.T, text_feat.T, text_head, pair_ids.reshape(256, B))
    loss, img_g, txt_g, head_g = pl.pallas_call(
        write_out,
        in_specs=[vm, vm],
        out_specs=[vm, vm, vm, vm],
        out_shape=[
            jax.ShapeDtypeStruct((1, B), f32),
            jax.ShapeDtypeStruct((D, B), f32),
            jax.ShapeDtypeStruct((D, B), f32),
            jax.ShapeDtypeStruct((D, D), f32),
        ],
        name="write_out",
    )(misc, res)
    return loss.reshape(B), img_g.T, txt_g.T, head_g


def solution(mesh):
    return jax.shard_map(
        shards,
        mesh=mesh,
        in_specs=(P(("group", "inner"), None), P(("group", "inner"), None), P(), P(), P(), P()),
        out_specs=(
            P(("group", "inner")),
            P(("group", "inner"), None),
            P(("group", "inner"), None),
            P(),
        ),
        check_vma=False,
    )
```
